256 devices in a mesh: chan: 32 (over x, z), rows: 8 (over y, core).
Axes of the slice: x: 4, y: 4, z: 8, core: 2. Of those that a mesh axis runs over, the one named last changes fastest.
Arguments:
- row_cells: int32 [256, 2048], P('chan', 'rows'), may hold values from 0 to 127
- col_cells: int32 [256, 2048], P('chan', 'rows'), may hold values from 0 to 2047
- visibilities: float32 [256, 2, 2048], P('chan', None, 'rows'), may hold values from -6 to 6
- imaging_weights: float32 [256, 2048], P('chan', 'rows'), may hold values from 0.05 to 1
- taylor_weights: float32 [256, 3], P('chan'), may hold values from -4 to 4
- kernel_taps: float32 [8], replicated, may hold values from 0.1 to 1
Outputs:
- normalized_grids: float32 [2048, 3, 2, 1024], P('chan', None, None, 'rows')
The draws below stay inside these ranges and needn't reach their ends.
Inputs may be any that keep to these rules, and one draw needn't show every extreme that they name: `row_cells`: a visibility's centre row within its slab.
All inputs are finite; a program needn't handle non-finite values.
Results may differ from the reference program's by a relative error of at most 0.0041.
Values sent between devices are 32-bit elements; how exact they have to be, the bound alone decides.
A program may use at most 384 MiB of HBM per device.

```python
import math
import jax
import jax.numpy as jnp
from jax import lax

NCOL = 2048
TERMS = 3
SUPPORT = 8
ROWS_DEV = 128
NV_DEV = 256
CHANNELS = 256
NVIS = 2048
NROW = 1024


def with_ends(entries, key, low, high):
    spot = [jax.random.randint(jax.random.fold_in(key, axis), (), 0, length) for axis, length in enumerate(entries.shape)]
    main_axis = entries.shape.index(max(entries.shape))
    next_to = spot[:main_axis] + [(spot[main_axis] + 1) % entries.shape[main_axis]] + spot[main_axis + 1:]
    return entries.at[tuple(spot)].set(low).at[tuple(next_to)].set(high)


def steps_of(key, shape, cuts, smallest, largest):
    loudness = 1.0
    for dim, shards_of in cuts:
        steps = jax.random.uniform(jax.random.fold_in(jax.random.fold_in(key, 6), dim), (shards_of,), jnp.float32, smallest / len(cuts), largest / len(cuts))
        loudness = loudness * jnp.repeat(jnp.exp(steps), shape[dim] // shards_of).reshape((-1,) + (1,) * (len(shape) - 1 - dim))
    return loudness


def scatter_about(own_key, extent, scale, most, split=(), held_as=jnp.bfloat16):
    entries = scale * jax.random.normal(own_key, extent, jnp.float32)
    if split:
        entries = entries * steps_of(own_key, extent, split, -0.22, 0.18)
    return jnp.clip(entries, -most, most).astype(held_as)


def setup_inputs(seed: int = 0) -> dict:
    splits = jax.random.split(jax.random.key(seed), 7)
    return {
        "row_cells": with_ends(jax.random.randint(splits[0], (CHANNELS, NVIS), 0, ROWS_DEV), jax.random.fold_in(splits[0], 1), 0, ROWS_DEV - 1).astype(jnp.int32),
        "col_cells": with_ends(jax.random.randint(splits[1], (CHANNELS, NVIS), 0, NCOL), jax.random.fold_in(splits[1], 1), 0, NCOL - 1).astype(jnp.int32),
        "visibilities": scatter_about(splits[2], (CHANNELS, 2, NVIS), 1.0, 6.0, ((0, 32), (2, 8)), jnp.float32),
        "imaging_weights": jnp.clip(jnp.exp(math.log(1.0) - 2.9957323 * jax.random.uniform(splits[3], (CHANNELS, NVIS), jnp.float32) ** steps_of(splits[3], (CHANNELS, NVIS), ((0, 32), (1, 8)), -0.2, 0.2)), 0.05, 1.0),
        "taylor_weights": scatter_about(splits[4], (CHANNELS, TERMS), 1.0, 4.0, ((0, 32),), jnp.float32),
        "kernel_taps": jnp.clip(jnp.exp(jax.random.uniform(splits[5], (SUPPORT,), jnp.float32, math.log(0.1), math.log(1.0))), 0.1, 1.0),
    }


def invert_three(matrix):
    first_row = matrix[0]
    second_row = matrix[1]
    third_row = matrix[2]
    across = jnp.stack([jnp.cross(second_row, third_row), jnp.cross(third_row, first_row), jnp.cross(first_row, second_row)], axis=1)
    determinant = jnp.sum(first_row * across[:, 0])
    return across / determinant


def reference(row_cells, col_cells, visibilities, imaging_weights, taylor_weights, kernel_taps):
    centre = SUPPORT // 2
    taps_round = kernel_taps.astype(jnp.bfloat16).astype(jnp.float32)
    slab_base = (jnp.arange(NVIS, dtype=jnp.int32) // NV_DEV) * ROWS_DEV
    scaled = taylor_weights[:, :, None, None] * (imaging_weights[:, None, None, :] * visibilities[:, None, :, :])
    scaled = jnp.transpose(scaled, (0, 3, 1, 2)).reshape(CHANNELS, NVIS, TERMS * 2)
    gridded = jnp.zeros((NROW, NCOL, TERMS * 2), jnp.float32)
    for row_tap in range(SUPPORT):
        row_here = row_cells + (row_tap - centre)
        inside_row = (row_here >= 0) & (row_here < ROWS_DEV)
        values = (scaled * kernel_taps[row_tap]).astype(jnp.bfloat16).astype(jnp.float32)
        row_global = (jnp.clip(row_here, 0, ROWS_DEV - 1) + slab_base[None, :]).astype(jnp.int32)
        for col_tap in range(SUPPORT):
            col_here = col_cells + (col_tap - centre)
            inside = inside_row & (col_here >= 0) & (col_here < NCOL)
            contrib = jnp.where(inside[:, :, None], values * taps_round[col_tap], jnp.float32(0.0))
            col_index = jnp.clip(col_here, 0, NCOL - 1).astype(jnp.int32)
            gridded = gridded.at[row_global.reshape(-1), col_index.reshape(-1)].add(contrib.reshape(-1, TERMS * 2))
    gridded = gridded.reshape(NROW, NCOL, TERMS, 2)
    chan_sum = jnp.sum(imaging_weights, axis=1)
    hessian = jnp.einsum('ca,cb,c->ab', taylor_weights, taylor_weights, chan_sum, precision=lax.Precision.HIGHEST)
    inverse = invert_three(hessian / hessian[0, 0])
    return jnp.einsum('ab,rcbi->cair', inverse, gridded, precision=lax.Precision.HIGHEST)
```

```python
import functools

import jax
import jax.numpy as jnp
from jax import lax
from jax.experimental import pallas as pl
from jax.experimental.pallas import tpu as pltpu
from jax.sharding import PartitionSpec as P

NCOL = 2048
TERMS = 3
ROWS_DEV = 128
SUPPORT = 8
CENTRE = SUPPORT // 2
SLOTS = 128
PAIRS = ((0, 0), (0, 1), (0, 2), (1, 1), (1, 2), (2, 2))
ACROSS_X, ACROSS_Z = 4, 8
HALF = 48
PER_STEP = 4

MESH = pl.DeviceIdType.MESH
F32 = jnp.float32
BF16 = jnp.bfloat16


def ring_distance(step, length):
    return min(step % length, -step % length)


def near_first():
    steps = [(x, z) for x in range(ACROSS_X) for z in range(ACROSS_Z)]
    return sorted(steps, key=lambda s: (ring_distance(s[0], ACROSS_X) + ring_distance(s[1], ACROSS_Z), s))


def matmul_nt(a, b):
    return lax.dot_general(a, b, (((1,), (1,)), ((), ())), preferred_element_type=F32)


def matmul(a, b):
    return lax.dot_general(a, b, (((1,), (0,)), ((), ())), preferred_element_type=F32)


def iota(shape, axis):
    return lax.broadcasted_iota(jnp.int32, shape, axis)


def two_parts(value):
    high = value.astype(BF16)
    return high, (value - high.astype(F32)).astype(BF16)


def kernel(
    chans, n_rows, width,
    round_ref, row_ref, col_ref, vis_ref, weight_ref, taylor_ref, taps_ref,
    out_ref, rounds_ref,
    mine, theirs, a_ref, b_ref, e_ref, cells, mixed, hess_mine, hess_rows, hess_sum, hess_chan,
    send_sem, recv_sem, row_send, row_recv, hess_send, hess_recv,
):
    me, slab = lax.axis_index("chan"), lax.axis_index("rows")
    my_x, my_z = me // ACROSS_Z, me % ACROSS_Z
    steps = near_first()
    half = chans // 2
    n_chan = row_ref.shape[0]
    pieces = [(c, h) for c in range(n_chan) for h in range(2)]

    def partner(step):
        return ((my_x + step[0]) % ACROSS_X) * ACROSS_Z + (my_z + step[1]) % ACROSS_Z

    def place(owner):
        return (owner % 2) * half + owner // 2

    barrier = pltpu.get_barrier_semaphore()
    for step in steps[:0:-1]:
        pl.semaphore_signal(barrier, inc=1, device_id=(partner(step), slab), device_id_type=MESH)
    for i in range(1, n_rows):
        pl.semaphore_signal(barrier, inc=1, device_id=(me, (slab + i) % n_rows), device_id_type=MESH)

    col = col_ref[...].astype(F32)
    owner = iota((2 * half, 128), 0)
    owner = jnp.where(owner < half, 2 * owner, 2 * (owner - half) + 1)
    first = (owner * width - (SUPPORT - 1 - CENTRE)).astype(F32)
    reach = []
    for n, (c, h) in enumerate(pieces):
        at = col[c : c + 1, h * 128 : h * 128 + 128] - first
        inside = (at >= 0.0) & (at <= float(width + SUPPORT - 2))
        hit = jnp.where(inside, 1.0, 0.0)
        reach.append(hit)
        e_ref[n * 2 * half : (n + 1) * 2 * half, :] = hit.astype(BF16)
        at = jnp.where(inside, at, 0.0).astype(BF16)
        for par in range(2):
            a_ref[par, 13 * half : 14 * half, n * 128 : n * 128 + 128] = at[par * half : (par + 1) * half]
    before = jnp.where(iota((128, 256), 0) < iota((128, 256), 1), 1.0, 0.0).astype(BF16)
    counts = matmul(e_ref[...], before)
    start = jnp.zeros((2 * half, 128), F32)
    base = (round_ref[0] * SLOTS).astype(F32)
    slot = iota((SLOTS, 128), 0).astype(F32)
    for n in range(len(pieces)):
        now = counts[n * 2 * half : (n + 1) * 2 * half]
        rank = reach[n] * (now[:, :128] + start)
        start = start + now[:, 128:]
        for par in range(2):
            which = jnp.sum(rank[par * half : (par + 1) * half], axis=0, keepdims=True) - base
            b_ref[par, :, n * 128 : n * 128 + 128] = jnp.where(slot == which, 1.0, 0.0).astype(BF16)
    fullest = jnp.max(start, axis=0, keepdims=True)

    weight = weight_ref[...]
    taylor = taylor_ref[...]
    chan_sum = jnp.sum(weight, axis=1, keepdims=True)
    lane = iota((1, 128), 1)
    part = jnp.where(lane == len(PAIRS), fullest, 0.0)
    for i, (a, b) in enumerate(PAIRS):
        entry = jnp.sum(taylor[:, a : a + 1] * taylor[:, b : b + 1] * chan_sum, axis=0, keepdims=True)
        part = part + jnp.where(lane == i, entry, 0.0)

    def gather(values):
        return jnp.where(lane == len(PAIRS), jnp.max(values, axis=0), jnp.sum(values, axis=0))

    hess_mine[...] = part
    hess_rows[pl.ds(slab, 1)] = part[None]

    scaled = []
    for t in range(TERMS):
        for p in range(2):
            scaled.append(taylor[:, t : t + 1] * (weight * vis_ref[:, p, :]))
    rows = [two_parts(value) for value in scaled]
    rows = [high for high, _ in rows] + [low for _, low in rows] + [row_ref[...].astype(F32).astype(BF16)]
    rows = [value.astype(F32) for value in rows]
    for n, (c, h) in enumerate(pieces):
        hit = reach[n].astype(BF16)
        for i, value in enumerate(rows):
            spread = jnp.broadcast_to(value[c : c + 1, h * 128 : h * 128 + 128], (half, 128)).astype(BF16)
            for par in range(2):
                a_ref[par, i * half : (i + 1) * half, n * 128 : n * 128 + 128] = (
                    hit[par * half : (par + 1) * half] * spread
                )
    for par in range(2):
        tile = matmul_nt(a_ref[par], b_ref[par])
        for i in range(8):
            if i < 6:
                value = tile[i * half : (i + 1) * half] + tile[(6 + i) * half : (7 + i) * half]
            else:
                value = tile[(6 + i) * half : (7 + i) * half]
            mine[pl.ds(par * half * 8 + i, half, stride=8), :] = value

    pl.semaphore_wait(barrier, chans - 1 + n_rows - 1)
    row_copies = []
    for i in range(1, n_rows):
        to = (slab + i) % n_rows
        copy = pltpu.make_async_remote_copy(
            src_ref=hess_mine, dst_ref=hess_rows.at[slab], send_sem=row_send.at[i], recv_sem=row_recv.at[i],
            device_id=(me, to), device_id_type=MESH,
        )
        copy.start()
        row_copies.append(copy)
    copies = {}
    for step in steps[:0:-1]:
        to = partner(step)
        i = steps.index(step)
        copy = pltpu.make_async_remote_copy(
            src_ref=mine.at[pl.ds(pl.multiple_of(place(to) * 8, 8), 8)], dst_ref=theirs.at[i],
            send_sem=send_sem.at[i], recv_sem=recv_sem.at[i],
            device_id=(to, slab), device_id_type=MESH,
        )
        copy.start()
        copies[i] = copy
    theirs[0] = mine[pl.ds(pl.multiple_of(place(me) * 8, 8), 8), :]
    for copy in row_copies:
        copy.wait_recv()
    row_sum = gather(hess_rows[...])
    hess_sum[...] = row_sum
    hess_chan[0] = row_sum
    hess_copies = []
    for i in range(len(steps) - 1, 0, -1):
        copy = pltpu.make_async_remote_copy(
            src_ref=hess_sum, dst_ref=hess_chan.at[i], send_sem=hess_send.at[i], recv_sem=hess_recv.at[i],
            device_id=(partner(steps[i]), slab), device_id_type=MESH,
        )
        copy.start()
        hess_copies.append(copy)

    tap_of = iota((ROWS_DEV, ROWS_DEV), 1) - iota((ROWS_DEV, ROWS_DEV), 0) + CENTRE
    row_taps = jnp.zeros((ROWS_DEV, ROWS_DEV), F32)
    for k in range(SUPPORT):
        row_taps = jnp.where(tap_of == k, taps_ref[k], row_taps)
    row_high, row_low = two_parts(row_taps)

    half_cell = iota((HALF, 128), 0).astype(F32)
    row_cell = iota((2 * ROWS_DEV, 128), 0).astype(F32)
    for g in range(0, len(steps), PER_STEP):
        a_parts, b_parts = [], []
        for i in range(g, g + PER_STEP):
            if i > 0:
                copies[i].wait_recv()
            tile = theirs[i]
            high = tile.astype(BF16).astype(F32)
            low = tile - high
            at = tile[7:8]
            halves = jnp.floor(at * 0.5)
            key = tile[6:7] + (at - 2.0 * halves) * float(ROWS_DEV)
            b_parts.append(jnp.where(row_cell == key, 1.0, 0.0).astype(BF16))
            here = half_cell == halves
            a_parts.append(
                jnp.concatenate(
                    [jnp.where(here, part_of[v : v + 1], 0.0).astype(BF16) for part_of in (high, low) for v in range(6)],
                    axis=0,
                )
            )
        total = matmul_nt(jnp.concatenate(a_parts, axis=1), jnp.concatenate(b_parts, axis=1))
        if g == 0:
            cells[...] = total
        else:
            cells[...] += total

    for par in range(2):
        x = cells[: 6 * HALF, par * 128 : par * 128 + 128] + cells[6 * HALF :, par * 128 : par * 128 + 128]
        high, low = two_parts(x)
        mixed[par * 6 * HALF : (par + 1) * 6 * HALF, :] = (
            matmul(high, row_high) + matmul(low, row_high) + matmul(high, row_low)
        )

    for copy in hess_copies:
        copy.wait_recv()
    hess = gather(hess_chan[...])
    entries = {}
    for i, (a, b) in enumerate(PAIRS):
        entries[a, b] = entries[b, a] = jnp.sum(jnp.where(lane == i, hess, 0.0), axis=1, keepdims=True)
    scale = entries[0, 0]
    m = [[entries[a, b] / scale for b in range(3)] for a in range(3)]

    def cross(u, v):
        return [u[1] * v[2] - u[2] * v[1], u[2] * v[0] - u[0] * v[2], u[0] * v[1] - u[1] * v[0]]

    across = [cross(m[1], m[2]), cross(m[2], m[0]), cross(m[0], m[1])]
    det = m[0][0] * across[0][0] + m[0][1] * across[0][1] + m[0][2] * across[0][2]
    inverse = [[across[b][a] / det for b in range(3)] for a in range(3)]
    count = jnp.max(jnp.where(lane == len(PAIRS), hess, 0.0))
    rounds_ref[0] = (count.astype(jnp.int32) + (SLOTS - 1)) // SLOTS

    wide = width // 2
    col_taps = [jnp.full((8, 128), taps_ref[j], F32).astype(BF16).astype(F32)[:1] for j in range(SUPPORT)]
    for e in range(2):
        for p in range(2):
            grids = []
            for t in range(TERMS):
                grid = jnp.zeros((wide, 128), F32)
                for j in range(SUPPORT):
                    shift = e + SUPPORT - 1 - j
                    at = ((shift % 2) * 6 + t * 2 + p) * HALF + shift // 2
                    grid = grid + col_taps[j] * mixed[at : at + wide, :]
                grids.append(grid)
            for a in range(TERMS):
                value = inverse[a][0] * grids[0] + inverse[a][1] * grids[1] + inverse[a][2] * grids[2]
                out_ref[pl.ds(e * 6 + a * 2 + p, wide, stride=12), :] = value

    for copy in row_copies + hess_copies + list(copies.values()):
        copy.wait_send()


def grid_round(chans, n_rows, width, which, arrays):
    vmem, smem = pl.BlockSpec(memory_space=pltpu.VMEM), pl.BlockSpec(memory_space=pltpu.SMEM)
    n_vis = arrays[0].shape[0] * arrays[0].shape[1]
    return pl.pallas_call(
        functools.partial(kernel, chans, n_rows, width),
        out_shape=(
            jax.ShapeDtypeStruct((width * TERMS * 2, ROWS_DEV), F32),
            jax.ShapeDtypeStruct((1,), jnp.int32),
        ),
        in_specs=[smem] + [vmem] * 5 + [smem],
        out_specs=(vmem, smem),
        scratch_shapes=[
            pltpu.VMEM((chans * 8, SLOTS), F32),
            pltpu.VMEM((chans, 8, SLOTS), F32),
            pltpu.VMEM((2, 14 * chans // 2, n_vis), BF16),
            pltpu.VMEM((2, SLOTS, n_vis), BF16),
            pltpu.VMEM((n_vis // 128 * chans, 128), BF16),
            pltpu.VMEM((12 * HALF, 2 * ROWS_DEV), F32),
            pltpu.VMEM((12 * HALF, ROWS_DEV), F32),
            pltpu.VMEM((1, 128), F32),
            pltpu.VMEM((n_rows, 1, 128), F32),
            pltpu.VMEM((1, 128), F32),
            pltpu.VMEM((chans, 1, 128), F32),
            pltpu.SemaphoreType.DMA((chans,)),
            pltpu.SemaphoreType.DMA((chans,)),
            pltpu.SemaphoreType.DMA((n_rows,)),
            pltpu.SemaphoreType.DMA((n_rows,)),
            pltpu.SemaphoreType.DMA((chans,)),
            pltpu.SemaphoreType.DMA((chans,)),
        ],
        compiler_params=pltpu.CompilerParams(
            collective_id=0, has_side_effects=True, vmem_limit_bytes=40 * 1024 * 1024
        ),
    )(which, *arrays)


def body(*arrays):
    chans, n_rows = lax.axis_size("chan"), lax.axis_size("rows")
    width = NCOL // chans

    def more(state):
        return state[0] < state[1]

    def step(state):
        done, _, total = state
        part, rounds = grid_round(chans, n_rows, width, done[None], arrays)
        return done + 1, rounds[0], total + part

    part, rounds = grid_round(chans, n_rows, width, jnp.zeros((1,), jnp.int32), arrays)
    _, _, total = lax.while_loop(more, step, (jnp.int32(1), rounds[0], part))
    return total.reshape(width, TERMS, 2, ROWS_DEV)


def solution(mesh):
    in_specs = (
        P("chan", "rows"),
        P("chan", "rows"),
        P("chan", None, "rows"),
        P("chan", "rows"),
        P("chan", None),
        P(),
    )
    out_specs = P("chan", None, None, "rows")
    return jax.shard_map(body, mesh=mesh, in_specs=in_specs, out_specs=out_specs, check_vma=False)
```

```python
import functools

import jax
import jax.numpy as jnp
from jax import lax
from jax.experimental import pallas as pl
from jax.experimental.pallas import tpu as pltpu
from jax.sharding import PartitionSpec as P

NCOL = 2048
TERMS = 3
ROWS_DEV = 128
SUPPORT = 8
CENTRE = SUPPORT // 2
SLOTS = 127
PAIRS = ((0, 0), (0, 1), (0, 2), (1, 1), (1, 2), (2, 2))
ACROSS_X, ACROSS_Z = 4, 8
HALF = 48
PER_STEP = 4

MESH = pl.DeviceIdType.MESH
F32 = jnp.float32
BF16 = jnp.bfloat16
HBM = pltpu.HBM


def ring_distance(step, length):
    return min(step % length, -step % length)


def near_first():
    steps = [(x, z) for x in range(ACROSS_X) for z in range(ACROSS_Z)]
    return sorted(steps, key=lambda s: (ring_distance(s[0], ACROSS_X) + ring_distance(s[1], ACROSS_Z), s))


def matmul_nt(a, b):
    return lax.dot_general(a, b, (((1,), (1,)), ((), ())), preferred_element_type=F32)


def matmul(a, b):
    return lax.dot_general(a, b, (((1,), (0,)), ((), ())), preferred_element_type=F32)


def iota(shape, axis):
    return lax.broadcasted_iota(jnp.int32, shape, axis)


def two_parts(value):
    high = value.astype(BF16)
    return high, (value - high.astype(F32)).astype(BF16)


def kernel(
    chans, n_rows, width,
    round_hbm, row_hbm, col_hbm, vis_hbm, weight_hbm, taylor_hbm, taps_hbm,
    out_hbm, rounds_hbm,
    round_ref, row_ref, col_ref, vis_ref, weight_ref, taylor_ref, taps_ref, out_ref, rounds_ref,
    mine, theirs, a_ref, b_ref, e_ref, cells, mixed, hess_mine, hess_rows,
    in_sem, out_sem, rounds_sem, rows_here, chans_here, send_sem, recv_sem, row_send, row_recv,
):
    inputs = []
    for i, (src, dst) in enumerate((
        (weight_hbm, weight_ref), (taylor_hbm, taylor_ref), (col_hbm, col_ref), (round_hbm, round_ref),
        (vis_hbm, vis_ref), (row_hbm, row_ref), (taps_hbm, taps_ref),
    )):
        inputs.append(pltpu.make_async_copy(src, dst, in_sem.at[i]))
        inputs[-1].start()

    me, slab = lax.axis_index("chan"), lax.axis_index("rows")
    my_x, my_z = me // ACROSS_Z, me % ACROSS_Z
    my_y, core = slab // 2, slab % 2
    steps = near_first()
    half = chans // 2
    n_chan = row_ref.shape[0]
    pieces = [(c, h) for c in range(n_chan) for h in range(2)]

    def partner(step):
        return ((my_x + step[0]) % ACROSS_X) * ACROSS_Z + (my_z + step[1]) % ACROSS_Z

    def place(owner):
        return (owner % 2) * half + owner // 2

    barrier = pltpu.get_barrier_semaphore()
    for i in range(1, n_rows // 2):
        there = (my_y + i) % (n_rows // 2)
        pl.semaphore_signal(barrier, inc=1, device_id=(me, 2 * there), device_id_type=MESH)

    @pl.when(core == 1)
    def _():
        pl.semaphore_signal(barrier, inc=1, device_id=(me, 2 * my_y), device_id_type=MESH)

    for step in steps[:0:-1]:
        pl.semaphore_signal(barrier, inc=1, device_id=(partner(step), 2 * my_y + 1), device_id_type=MESH)

    inputs[0].wait()
    inputs[1].wait()
    weight = weight_ref[...]
    chan_sum = jnp.sum(weight, axis=1, keepdims=True)
    on_diagonal = iota((n_chan, n_chan), 0) == iota((n_chan, n_chan), 1)
    taylor = [
        jnp.sum(jnp.where(on_diagonal, taylor_ref[t : t + 1, :], 0.0), axis=1, keepdims=True) for t in range(TERMS)
    ]
    sublane = iota((8, 128), 0)
    part = jnp.zeros((8, 128), F32)
    for i, (a, b) in enumerate(PAIRS):
        entry = jnp.sum(taylor[a] * taylor[b] * chan_sum, axis=0, keepdims=True)
        part = jnp.where(sublane == i, entry, part)

    def gather(values):
        return jnp.where(sublane == len(PAIRS), jnp.max(values, axis=0), jnp.sum(values, axis=0))

    inputs[2].wait()
    inputs[3].wait()
    col = col_ref[...].astype(F32)
    owner = iota((2 * half, 128), 0)
    owner = jnp.where(owner < half, 2 * owner, 2 * (owner - half) + 1)
    first = (owner * width - (SUPPORT - 1 - CENTRE)).astype(F32)
    reach = []
    for n, (c, h) in enumerate(pieces):
        at = col[c : c + 1, h * 128 : h * 128 + 128] - first
        inside = (at >= 0.0) & (at <= float(width + SUPPORT - 2))
        hit = jnp.where(inside, 1.0, 0.0)
        reach.append(hit)
        e_ref[n * 2 * half : (n + 1) * 2 * half, :] = hit.astype(BF16)
        at = jnp.where(inside, at, 0.0).astype(BF16)
        for par in range(2):
            a_ref[par, 13 * half : 14 * half, n * 128 : n * 128 + 128] = at[par * half : (par + 1) * half]
    before = jnp.where(iota((128, 256), 0) < iota((128, 256), 1), 1.0, 0.0).astype(BF16)
    counts = matmul(e_ref[...], before)
    fullest = counts[: 2 * half, 128:]
    for n in range(1, len(pieces)):
        fullest = fullest + counts[n * 2 * half : (n + 1) * 2 * half, 128:]
    part = jnp.where(sublane == len(PAIRS), jnp.max(fullest, axis=0, keepdims=True), part)
    hess_mine[...] = part
    hess_rows[pl.ds(slab, 1)] = part[None]

    @pl.when(core == 0)
    def _():
        pl.semaphore_wait(barrier, n_rows - 1)
        pl.semaphore_signal(rows_here, inc=1, device_id=(me, slab + 1), device_id_type=MESH)

    @pl.when(core == 1)
    def _():
        pl.semaphore_wait(rows_here, 1)

    row_copies = []
    for i in range(1, n_rows):
        copy = pltpu.make_async_remote_copy(
            src_ref=hess_mine, dst_ref=hess_rows.at[slab], send_sem=row_send.at[i], recv_sem=row_recv.at[i],
            device_id=(me, (slab + i) % n_rows), device_id_type=MESH,
        )
        copy.start()
        row_copies.append(copy)

    start = jnp.zeros((2 * half, 128), F32)
    base = (round_ref[0] * SLOTS).astype(F32)
    slot = iota((128, 128), 0)
    slot = jnp.where(slot < SLOTS, slot.astype(F32), -0.5)
    for n in range(len(pieces)):
        now = counts[n * 2 * half : (n + 1) * 2 * half]
        rank = reach[n] * (now[:, :128] + start)
        start = start + now[:, 128:]
        for par in range(2):
            which = jnp.sum(rank[par * half : (par + 1) * half], axis=0, keepdims=True) - base
            b_ref[par, :, n * 128 : n * 128 + 128] = jnp.where(slot == which, 1.0, 0.0).astype(BF16)

    inputs[4].wait()
    inputs[5].wait()
    inputs[6].wait()
    scaled = []
    for t in range(TERMS):
        for p in range(2):
            scaled.append(taylor[t] * (weight * vis_ref[:, p, :]))
    rows = [two_parts(value) for value in scaled]
    rows = [high for high, _ in rows] + [low for _, low in rows] + [row_ref[...].astype(F32).astype(BF16)]
    rows = [value.astype(F32) for value in rows]
    for n, (c, h) in enumerate(pieces):
        hit = reach[n].astype(BF16)
        for i, value in enumerate(rows):
            spread = jnp.broadcast_to(value[c : c + 1, h * 128 : h * 128 + 128], (half, 128)).astype(BF16)
            for par in range(2):
                a_ref[par, i * half : (i + 1) * half, n * 128 : n * 128 + 128] = (
                    hit[par * half : (par + 1) * half] * spread
                )
    for par in range(2):
        tile = matmul_nt(a_ref[par], b_ref[par])
        for i in range(8):
            if i < 6:
                value = tile[i * half : (i + 1) * half] + tile[(6 + i) * half : (7 + i) * half]
            else:
                value = tile[(6 + i) * half : (7 + i) * half]
            mine[pl.ds(par * half * 8 + i, half, stride=8), :] = value

    for copy in row_copies:
        copy.wait_recv()
    row_sum = gather(hess_rows[...])
    last = iota((8, 128), 1) == SLOTS
    for i in range(chans):
        mine[i * 8 : i * 8 + 8, :] = jnp.where(last, row_sum, mine[i * 8 : i * 8 + 8, :])

    @pl.when(core == 1)
    def _():
        pl.semaphore_wait(barrier, 2 * (chans - 1))
        pl.semaphore_signal(chans_here, inc=1, device_id=(me, slab - 1), device_id_type=MESH)

    @pl.when(core == 0)
    def _():
        pl.semaphore_wait(chans_here, 1)

    copies = {}
    for i in range(len(steps) - 1, 0, -1):
        to = partner(steps[i])
        copies[i] = pltpu.make_async_remote_copy(
            src_ref=mine.at[pl.ds(pl.multiple_of(place(to) * 8, 8), 8)], dst_ref=theirs.at[i],
            send_sem=send_sem.at[i], recv_sem=recv_sem.at[i],
            device_id=(to, slab), device_id_type=MESH,
        )
        copies[i].start()
    theirs[0] = mine[pl.ds(pl.multiple_of(place(me) * 8, 8), 8), :]

    tap_of = iota((ROWS_DEV, ROWS_DEV), 1) - iota((ROWS_DEV, ROWS_DEV), 0) + CENTRE
    row_taps = jnp.zeros((ROWS_DEV, ROWS_DEV), F32)
    for k in range(SUPPORT):
        row_taps = jnp.where(tap_of == k, taps_ref[k], row_taps)
    row_high, row_low = two_parts(row_taps)

    half_cell = iota((HALF, 128), 0).astype(F32)
    row_cell = iota((2 * ROWS_DEV, 128), 0).astype(F32)
    for g in range(0, len(steps), PER_STEP):
        a_parts, b_parts = [], []
        for i in range(g, g + PER_STEP):
            if i > 0:
                copies[i].wait_recv()
            tile = theirs[i]
            sums = tile if i == 0 else sums + tile
            most = tile if i == 0 else jnp.maximum(most, tile)
            tile = jnp.where(last, 0.0, tile)
            high = tile.astype(BF16).astype(F32)
            low = tile - high
            at = tile[7:8]
            halves = jnp.floor(at * 0.5)
            key = tile[6:7] + (at - 2.0 * halves) * float(ROWS_DEV)
            b_parts.append(jnp.where(row_cell == key, 1.0, 0.0).astype(BF16))
            here = half_cell == halves
            a_parts.append(
                jnp.concatenate(
                    [jnp.where(here, part_of[v : v + 1], 0.0).astype(BF16) for part_of in (high, low) for v in range(6)],
                    axis=0,
                )
            )
        total = matmul_nt(jnp.concatenate(a_parts, axis=1), jnp.concatenate(b_parts, axis=1))
        if g == 0:
            cells[...] = total
        else:
            cells[...] += total

    for par in range(2):
        x = cells[: 6 * HALF, par * 128 : par * 128 + 128] + cells[6 * HALF :, par * 128 : par * 128 + 128]
        high, low = two_parts(x)
        mixed[par * 6 * HALF : (par + 1) * 6 * HALF, :] = (
            matmul(high, row_high) + matmul(low, row_high) + matmul(high, row_low)
        )

    entries = {}
    for i, (a, b) in enumerate(PAIRS):
        entries[a, b] = entries[b, a] = sums[i : i + 1, SLOTS : SLOTS + 1]
    scale = entries[0, 0]
    m = [[entries[a, b] / scale for b in range(3)] for a in range(3)]

    def cross(u, v):
        return [u[1] * v[2] - u[2] * v[1], u[2] * v[0] - u[0] * v[2], u[0] * v[1] - u[1] * v[0]]

    across = [cross(m[1], m[2]), cross(m[2], m[0]), cross(m[0], m[1])]
    det = m[0][0] * across[0][0] + m[0][1] * across[0][1] + m[0][2] * across[0][2]
    inverse = [[across[b][a] / det for b in range(3)] for a in range(3)]
    count = jnp.max(jnp.where(last & (sublane == len(PAIRS)), most, 0.0))
    rounds_ref[0] = (count.astype(jnp.int32) + (SLOTS - 1)) // SLOTS
    rounds_copy = pltpu.make_async_copy(rounds_ref, rounds_hbm, rounds_sem)
    rounds_copy.start()

    wide = width // 2
    col_taps = [jnp.full((8, 128), taps_ref[j], F32).astype(BF16).astype(F32)[:1] for j in range(SUPPORT)]
    for e in range(2):
        for p in range(2):
            grids = []
            for t in range(TERMS):
                grid = jnp.zeros((wide, 128), F32)
                for j in range(SUPPORT):
                    shift = e + SUPPORT - 1 - j
                    at = ((shift % 2) * 6 + t * 2 + p) * HALF + shift // 2
                    grid = grid + col_taps[j] * mixed[at : at + wide, :]
                grids.append(grid)
            for a in range(TERMS):
                value = inverse[a][0] * grids[0] + inverse[a][1] * grids[1] + inverse[a][2] * grids[2]
                out_ref[pl.ds(e * 6 + a * 2 + p, wide, stride=12), :] = value

    out_copy = pltpu.make_async_copy(out_ref, out_hbm, out_sem)
    out_copy.start()
    for copy in row_copies + list(copies.values()):
        copy.wait_send()
    rounds_copy.wait()
    out_copy.wait()


def grid_round(chans, n_rows, width, which, arrays):
    hbm = pl.BlockSpec(memory_space=HBM)
    n_vis = arrays[0].shape[0] * arrays[0].shape[1]
    out = jax.ShapeDtypeStruct((width * TERMS * 2, ROWS_DEV), F32)
    return pl.pallas_call(
        functools.partial(kernel, chans, n_rows, width),
        out_shape=(out, jax.ShapeDtypeStruct((1,), jnp.int32)),
        in_specs=[hbm] * 7,
        out_specs=(hbm, hbm),
        scratch_shapes=[
            pltpu.SMEM((1,), jnp.int32),
            *[pltpu.VMEM(a.shape, a.dtype) for a in arrays[:-1]],
            pltpu.SMEM(arrays[-1].shape, F32),
            pltpu.VMEM(out.shape, F32),
            pltpu.SMEM((1,), jnp.int32),
            pltpu.VMEM((chans * 8, 128), F32),
            pltpu.VMEM((chans, 8, 128), F32),
            pltpu.VMEM((2, 14 * chans // 2, n_vis), BF16),
            pltpu.VMEM((2, 128, n_vis), BF16),
            pltpu.VMEM((n_vis // 128 * chans, 128), BF16),
            pltpu.VMEM((12 * HALF, 2 * ROWS_DEV), F32),
            pltpu.VMEM((12 * HALF, ROWS_DEV), F32),
            pltpu.VMEM((8, 128), F32),
            pltpu.VMEM((n_rows, 8, 128), F32),
            pltpu.SemaphoreType.DMA((7,)),
            pltpu.SemaphoreType.DMA,
            pltpu.SemaphoreType.DMA,
            pltpu.SemaphoreType.REGULAR,
            pltpu.SemaphoreType.REGULAR,
            pltpu.SemaphoreType.DMA((chans,)),
            pltpu.SemaphoreType.DMA((chans,)),
            pltpu.SemaphoreType.DMA((n_rows,)),
            pltpu.SemaphoreType.DMA((n_rows,)),
        ],
        compiler_params=pltpu.CompilerParams(
            collective_id=0, has_side_effects=True, vmem_limit_bytes=40 * 1024 * 1024
        ),
    )(which, *arrays)


def body(row_cells, col_cells, visibilities, imaging_weights, taylor_weights, kernel_taps):
    arrays = (row_cells, col_cells, visibilities, imaging_weights, taylor_weights.T, kernel_taps)
    chans, n_rows = lax.axis_size("chan"), lax.axis_size("rows")
    width = NCOL // chans

    def more(state):
        return state[0] < state[1]

    def step(state):
        done, _, total = state
        part, rounds = grid_round(chans, n_rows, width, done[None], arrays)
        return done + 1, rounds[0], total + part

    part, rounds = grid_round(chans, n_rows, width, jnp.zeros((1,), jnp.int32), arrays)
    _, _, total = lax.while_loop(more, step, (jnp.int32(1), rounds[0], part))
    return total.reshape(width, TERMS, 2, ROWS_DEV)


def solution(mesh):
    in_specs = (
        P("chan", "rows"),
        P("chan", "rows"),
        P("chan", None, "rows"),
        P("chan", "rows"),
        P("chan", None),
        P(),
    )
    out_specs = P("chan", None, None, "rows")
    return jax.shard_map(body, mesh=mesh, in_specs=in_specs, out_specs=out_specs, check_vma=False)
```

```python
import functools

import jax
import jax.numpy as jnp
from jax import lax
from jax.experimental import pallas as pl
from jax.experimental.pallas import tpu as pltpu
from jax.sharding import PartitionSpec as P

NCOL = 2048
TERMS = 3
ROWS_DEV = 128
SUPPORT = 8
CENTRE = SUPPORT // 2
SLOTS = 127
PAIRS = ((0, 0), (0, 1), (0, 2), (1, 1), (1, 2), (2, 2))
ACROSS_X, ACROSS_Z = 4, 8
Z_ORDER = (0, 1, 2, 3, 7, 6, 5, 4)
HALF = 48
PER_STEP = 4

MESH = pl.DeviceIdType.MESH
F32 = jnp.float32
BF16 = jnp.bfloat16
HBM = pltpu.HBM


def in_order_of_start():
    return [x * ACROSS_Z + z for z in Z_ORDER for x in range(ACROSS_X)]


def matmul_nt(a, b):
    return lax.dot_general(a, b, (((1,), (1,)), ((), ())), preferred_element_type=F32)


def matmul(a, b):
    return lax.dot_general(a, b, (((1,), (0,)), ((), ())), preferred_element_type=F32)


def iota(shape, axis):
    return lax.broadcasted_iota(jnp.int32, shape, axis)


def two_parts(value):
    high = value.astype(BF16)
    return high, (value - high.astype(F32)).astype(BF16)


def kernel(
    chans, n_rows, width,
    round_hbm, row_hbm, col_hbm, vis_hbm, weight_hbm, taylor_hbm, taps_hbm,
    out_ref, rounds_ref,
    round_ref, row_ref, col_ref, vis_ref, weight_ref, taylor_ref, taps_ref,
    mine, theirs, a_ref, b_ref, e_ref, cells, mixed, hess_mine, hess_rows,
    in_sem, rows_here, chans_here, send_sem, recv_sem, row_send, row_recv,
):
    inputs = []
    for i, (src, dst) in enumerate((
        (weight_hbm, weight_ref), (taylor_hbm, taylor_ref), (col_hbm, col_ref), (round_hbm, round_ref),
        (vis_hbm, vis_ref), (row_hbm, row_ref), (taps_hbm, taps_ref),
    )):
        inputs.append(pltpu.make_async_copy(src, dst, in_sem.at[i]))
        inputs[-1].start()

    me, slab = lax.axis_index("chan"), lax.axis_index("rows")
    my_y, core = slab // 2, slab % 2
    chips = in_order_of_start()
    half = chans // 2
    n_chan = row_ref.shape[0]
    pieces = [(c, h) for c in range(n_chan) for h in range(2)]

    def place(owner):
        return (owner % 2) * half + owner // 2

    barrier = pltpu.get_barrier_semaphore()
    for i in range(1, n_rows // 2):
        there = (my_y + i) % (n_rows // 2)
        pl.semaphore_signal(barrier, inc=1, device_id=(me, 2 * there), device_id_type=MESH)

    @pl.when(core == 1)
    def _():
        pl.semaphore_signal(barrier, inc=1, device_id=(me, 2 * my_y), device_id_type=MESH)

    for chip in chips:

        @pl.when(chip != me)
        def _(chip=chip):
            pl.semaphore_signal(barrier, inc=1, device_id=(chip, 2 * my_y + 1), device_id_type=MESH)

    inputs[0].wait()
    inputs[1].wait()
    weight = weight_ref[...]
    chan_sum = jnp.sum(weight, axis=1, keepdims=True)
    on_diagonal = iota((n_chan, n_chan), 0) == iota((n_chan, n_chan), 1)
    taylor = [
        jnp.sum(jnp.where(on_diagonal, taylor_ref[t : t + 1, :], 0.0), axis=1, keepdims=True) for t in range(TERMS)
    ]
    sublane = iota((8, 128), 0)
    part = jnp.zeros((8, 128), F32)
    for i, (a, b) in enumerate(PAIRS):
        entry = jnp.sum(taylor[a] * taylor[b] * chan_sum, axis=0, keepdims=True)
        part = jnp.where(sublane == i, entry, part)

    def gather(values):
        return jnp.where(sublane == len(PAIRS), jnp.max(values, axis=0), jnp.sum(values, axis=0))

    inputs[2].wait()
    inputs[3].wait()
    col = col_ref[...].astype(F32)
    owner = iota((2 * half, 128), 0)
    owner = jnp.where(owner < half, 2 * owner, 2 * (owner - half) + 1)
    first = (owner * width - (SUPPORT - 1 - CENTRE)).astype(F32)
    reach = []
    for n, (c, h) in enumerate(pieces):
        at = col[c : c + 1, h * 128 : h * 128 + 128] - first
        inside = (at >= 0.0) & (at <= float(width + SUPPORT - 2))
        hit = jnp.where(inside, 1.0, 0.0)
        reach.append(hit)
        e_ref[n * 2 * half : (n + 1) * 2 * half, :] = hit.astype(BF16)
        at = jnp.where(inside, at, 0.0).astype(BF16)
        for par in range(2):
            a_ref[par, 13 * half : 14 * half, n * 128 : n * 128 + 128] = at[par * half : (par + 1) * half]
    before = jnp.where(iota((128, 256), 0) < iota((128, 256), 1), 1.0, 0.0).astype(BF16)
    counts = matmul(e_ref[...], before)
    fullest = counts[: 2 * half, 128:]
    for n in range(1, len(pieces)):
        fullest = fullest + counts[n * 2 * half : (n + 1) * 2 * half, 128:]
    part = jnp.where(sublane == len(PAIRS), jnp.max(fullest, axis=0, keepdims=True), part)
    hess_mine[...] = part
    hess_rows[pl.ds(slab, 1)] = part[None]

    @pl.when(core == 0)
    def _():
        pl.semaphore_wait(barrier, n_rows - 1)
        pl.semaphore_signal(rows_here, inc=1, device_id=(me, slab + 1), device_id_type=MESH)

    @pl.when(core == 1)
    def _():
        pl.semaphore_wait(rows_here, 1)

    row_copies = []
    for i in range(1, n_rows):
        copy = pltpu.make_async_remote_copy(
            src_ref=hess_mine, dst_ref=hess_rows.at[slab], send_sem=row_send.at[i], recv_sem=row_recv.at[i],
            device_id=(me, (slab + i) % n_rows), device_id_type=MESH,
        )
        copy.start()
        row_copies.append(copy)

    start = jnp.zeros((2 * half, 128), F32)
    base = (round_ref[0] * SLOTS).astype(F32)
    slot = iota((128, 128), 0)
    slot = jnp.where(slot < SLOTS, slot.astype(F32), -0.5)
    for n in range(len(pieces)):
        now = counts[n * 2 * half : (n + 1) * 2 * half]
        rank = reach[n] * (now[:, :128] + start)
        start = start + now[:, 128:]
        for par in range(2):
            which = jnp.sum(rank[par * half : (par + 1) * half], axis=0, keepdims=True) - base
            b_ref[par, :, n * 128 : n * 128 + 128] = jnp.where(slot == which, 1.0, 0.0).astype(BF16)

    inputs[4].wait()
    inputs[5].wait()
    inputs[6].wait()
    scaled = []
    for t in range(TERMS):
        for p in range(2):
            scaled.append(taylor[t] * (weight * vis_ref[:, p, :]))
    rows = [two_parts(value) for value in scaled]
    rows = [high for high, _ in rows] + [low for _, low in rows] + [row_ref[...].astype(F32).astype(BF16)]
    rows = [value.astype(F32) for value in rows]
    for n, (c, h) in enumerate(pieces):
        hit = reach[n].astype(BF16)
        for i, value in enumerate(rows):
            spread = jnp.broadcast_to(value[c : c + 1, h * 128 : h * 128 + 128], (half, 128)).astype(BF16)
            for par in range(2):
                a_ref[par, i * half : (i + 1) * half, n * 128 : n * 128 + 128] = (
                    hit[par * half : (par + 1) * half] * spread
                )
    for par in range(2):
        tile = matmul_nt(a_ref[par], b_ref[par])
        for i in range(8):
            if i < 6:
                value = tile[i * half : (i + 1) * half] + tile[(6 + i) * half : (7 + i) * half]
            else:
                value = tile[(6 + i) * half : (7 + i) * half]
            mine[pl.ds(par * half * 8 + i, half, stride=8), :] = value

    for copy in row_copies:
        copy.wait_recv()
    row_sum = gather(hess_rows[...])
    last = iota((8, 128), 1) == SLOTS
    for i in range(chans):
        mine[i * 8 : i * 8 + 8, :] = jnp.where(last, row_sum, mine[i * 8 : i * 8 + 8, :])

    @pl.when(core == 1)
    def _():
        pl.semaphore_wait(barrier, 2 * (chans - 1))
        pl.semaphore_signal(chans_here, inc=1, device_id=(me, slab - 1), device_id_type=MESH)

    @pl.when(core == 0)
    def _():
        pl.semaphore_wait(chans_here, 1)

    def tile_to(owner):
        return pltpu.make_async_remote_copy(
            src_ref=mine.at[pl.ds(place(owner) * 8, 8)], dst_ref=theirs.at[me],
            send_sem=send_sem.at[owner], recv_sem=recv_sem.at[me],
            device_id=(owner, slab), device_id_type=MESH,
        )

    def tile_from(sender):
        return pltpu.make_async_remote_copy(
            src_ref=mine.at[pl.ds(0, 8)], dst_ref=theirs.at[sender],
            send_sem=send_sem.at[sender], recv_sem=recv_sem.at[sender],
            device_id=(sender, slab), device_id_type=MESH,
        )

    for chip in chips:

        @pl.when(chip != me)
        def _(chip=chip):
            tile_to(chip).start()

    theirs[me] = mine[pl.ds(pl.multiple_of(place(me) * 8, 8), 8), :]

    tap_of = iota((ROWS_DEV, ROWS_DEV), 1) - iota((ROWS_DEV, ROWS_DEV), 0) + CENTRE
    row_taps = jnp.zeros((ROWS_DEV, ROWS_DEV), F32)
    for k in range(SUPPORT):
        row_taps = jnp.where(tap_of == k, taps_ref[k], row_taps)
    row_high, row_low = two_parts(row_taps)

    half_cell = iota((HALF, 128), 0).astype(F32)
    row_cell = iota((2 * ROWS_DEV, 128), 0).astype(F32)
    for g in range(0, chans, PER_STEP):
        a_parts, b_parts = [], []
        for chip in chips[g : g + PER_STEP]:

            @pl.when(chip != me)
            def _(chip=chip):
                tile_from(chip).wait_recv()

        for i in chips[g : g + PER_STEP]:
            tile = theirs[i]
            sums = tile if i == chips[0] else sums + tile
            most = tile if i == chips[0] else jnp.maximum(most, tile)
            tile = jnp.where(last, 0.0, tile)
            high = tile.astype(BF16).astype(F32)
            low = tile - high
            at = tile[7:8]
            halves = jnp.floor(at * 0.5)
            key = tile[6:7] + (at - 2.0 * halves) * float(ROWS_DEV)
            b_parts.append(jnp.where(row_cell == key, 1.0, 0.0).astype(BF16))
            here = half_cell == halves
            a_parts.append(
                jnp.concatenate(
                    [jnp.where(here, part_of[v : v + 1], 0.0).astype(BF16) for part_of in (high, low) for v in range(6)],
                    axis=0,
                )
            )
        total = matmul_nt(jnp.concatenate(a_parts, axis=1), jnp.concatenate(b_parts, axis=1))
        if g == 0:
            cells[...] = total
        else:
            cells[...] += total

    for par in range(2):
        x = cells[: 6 * HALF, par * 128 : par * 128 + 128] + cells[6 * HALF :, par * 128 : par * 128 + 128]
        high, low = two_parts(x)
        mixed[par * 6 * HALF : (par + 1) * 6 * HALF, :] = (
            matmul(high, row_high) + matmul(low, row_high) + matmul(high, row_low)
        )

    entries = {}
    for i, (a, b) in enumerate(PAIRS):
        entries[a, b] = entries[b, a] = sums[i : i + 1, SLOTS : SLOTS + 1]
    scale = entries[0, 0]
    m = [[entries[a, b] / scale for b in range(3)] for a in range(3)]

    def cross(u, v):
        return [u[1] * v[2] - u[2] * v[1], u[2] * v[0] - u[0] * v[2], u[0] * v[1] - u[1] * v[0]]

    across = [cross(m[1], m[2]), cross(m[2], m[0]), cross(m[0], m[1])]
    det = m[0][0] * across[0][0] + m[0][1] * across[0][1] + m[0][2] * across[0][2]
    inverse = [[across[b][a] / det for b in range(3)] for a in range(3)]
    count = jnp.max(jnp.where(last & (sublane == len(PAIRS)), most, 0.0))
    rounds_ref[0] = (count.astype(jnp.int32) + (SLOTS - 1)) // SLOTS

    wide = width // 2
    col_taps = [jnp.full((8, 128), taps_ref[j], F32).astype(BF16).astype(F32)[:1] for j in range(SUPPORT)]
    for e in range(2):
        for p in range(2):
            grids = []
            for t in range(TERMS):
                grid = jnp.zeros((wide, 128), F32)
                for j in range(SUPPORT):
                    shift = e + SUPPORT - 1 - j
                    at = ((shift % 2) * 6 + t * 2 + p) * HALF + shift // 2
                    grid = grid + col_taps[j] * mixed[at : at + wide, :]
                grids.append(grid)
            for a in range(TERMS):
                value = inverse[a][0] * grids[0] + inverse[a][1] * grids[1] + inverse[a][2] * grids[2]
                out_ref[pl.ds(e * 6 + a * 2 + p, wide, stride=12), :] = value

    for copy in row_copies:
        copy.wait_send()
    for chip in chips:

        @pl.when(chip != me)
        def _(chip=chip):
            tile_to(chip).wait_send()


def grid_round(chans, n_rows, width, which, arrays):
    hbm = pl.BlockSpec(memory_space=HBM)
    n_vis = arrays[0].shape[0] * arrays[0].shape[1]
    out = jax.ShapeDtypeStruct((width * TERMS * 2, ROWS_DEV), F32)
    return pl.pallas_call(
        functools.partial(kernel, chans, n_rows, width),
        out_shape=(pltpu.VMEM(out.shape, F32), pltpu.SMEM((1,), jnp.int32)),
        in_specs=[hbm] * 7,
        out_specs=(pl.BlockSpec(memory_space=pltpu.VMEM), pl.BlockSpec(memory_space=pltpu.SMEM)),
        scratch_shapes=[
            pltpu.SMEM((1,), jnp.int32),
            *[pltpu.VMEM(a.shape, a.dtype) for a in arrays[:-1]],
            pltpu.SMEM(arrays[-1].shape, F32),
            pltpu.VMEM((chans * 8, 128), F32),
            pltpu.VMEM((chans, 8, 128), F32),
            pltpu.VMEM((2, 14 * chans // 2, n_vis), BF16),
            pltpu.VMEM((2, 128, n_vis), BF16),
            pltpu.VMEM((n_vis // 128 * chans, 128), BF16),
            pltpu.VMEM((12 * HALF, 2 * ROWS_DEV), F32),
            pltpu.VMEM((12 * HALF, ROWS_DEV), F32),
            pltpu.VMEM((8, 128), F32),
            pltpu.VMEM((n_rows, 8, 128), F32),
            pltpu.SemaphoreType.DMA((7,)),
            pltpu.SemaphoreType.REGULAR,
            pltpu.SemaphoreType.REGULAR,
            pltpu.SemaphoreType.DMA((chans,)),
            pltpu.SemaphoreType.DMA((chans,)),
            pltpu.SemaphoreType.DMA((n_rows,)),
            pltpu.SemaphoreType.DMA((n_rows,)),
        ],
        compiler_params=pltpu.CompilerParams(
            collective_id=0, has_side_effects=True, vmem_limit_bytes=40 * 1024 * 1024
        ),
    )(*[pltpu.with_memory_space_constraint(a, HBM) for a in (which, *arrays)])


def body(row_cells, col_cells, visibilities, imaging_weights, taylor_weights, kernel_taps):
    arrays = (row_cells, col_cells, visibilities, imaging_weights, taylor_weights.T, kernel_taps)
    chans, n_rows = lax.axis_size("chan"), lax.axis_size("rows")
    width = NCOL // chans

    def more(state):
        return state[0] < state[1]

    def step(state):
        done, _, total = state
        part, rounds = grid_round(chans, n_rows, width, done[None], arrays)
        return done + 1, rounds[0], total + part

    part, rounds = grid_round(chans, n_rows, width, jnp.zeros((1,), jnp.int32), arrays)
    _, _, total = lax.while_loop(more, step, (jnp.int32(1), rounds[0], part))
    return total.reshape(width, TERMS, 2, ROWS_DEV)


def solution(mesh):
    in_specs = (
        P("chan", "rows"),
        P("chan", "rows"),
        P("chan", None, "rows"),
        P("chan", "rows"),
        P("chan", None),
        P(),
    )
    out_specs = P("chan", None, None, "rows")
    return jax.shard_map(body, mesh=mesh, in_specs=in_specs, out_specs=out_specs, check_vma=False)
```

```python
import functools

import jax
import jax.numpy as jnp
from jax import lax
from jax.experimental import pallas as pl
from jax.experimental.pallas import tpu as pltpu
from jax.sharding import PartitionSpec as P

NCOL = 2048
TERMS = 3
ROWS_DEV = 128
SUPPORT = 8
CENTRE = SUPPORT // 2
SLOTS = 128
PAIRS = ((0, 0), (0, 1), (0, 2), (1, 1), (1, 2), (2, 2))
ACROSS_X, ACROSS_Z = 4, 8
Z_ORDER = (0, 1, 2, 3, 7, 6, 5, 4)
EARLY = 3
HALF = 48
PER_STEP = 4

MESH = pl.DeviceIdType.MESH
F32 = jnp.float32
BF16 = jnp.bfloat16
HBM = pltpu.HBM


def in_order_of_start():
    return [x * ACROSS_Z + z for z in Z_ORDER for x in range(ACROSS_X)]


def matmul_nt(a, b):
    return lax.dot_general(a, b, (((1,), (1,)), ((), ())), preferred_element_type=F32)


def matmul(a, b):
    return lax.dot_general(a, b, (((1,), (0,)), ((), ())), preferred_element_type=F32)


def iota(shape, axis):
    return lax.broadcasted_iota(jnp.int32, shape, axis)


def two_parts(value):
    high = value.astype(BF16)
    return high, (value - high.astype(F32)).astype(BF16)


def kernel(
    chans, n_rows, width,
    round_hbm, row_hbm, col_hbm, vis_hbm, weight_hbm, taylor_hbm, taps_hbm,
    out_ref, rounds_ref,
    round_ref, row_ref, col_ref, vis_ref, weight_ref, taylor_ref, taps_ref,
    mine, theirs, a_ref, b_ref, e_ref, cells, mixed, grids, hess_mine, hess_chan, hess_sum, hess_rows,
    in_sem, early_here, late_here, send_sem, recv_sem, row_send, row_recv, hess_send, hess_recv,
):
    me, slab = lax.axis_index("chan"), lax.axis_index("rows")
    my_y, core = slab // 2, slab % 2
    chips = in_order_of_start()
    half = chans // 2
    n_chan = row_ref.shape[0]
    pieces = [(c, h) for c in range(n_chan) for h in range(2)]

    def place(owner):
        return (owner % 2) * half + owner // 2

    inputs = []
    for i, (src, dst) in enumerate((
        (col_hbm, col_ref), (round_hbm, round_ref), (weight_hbm, weight_ref), (taylor_hbm, taylor_ref),
        (vis_hbm, vis_ref), (row_hbm, row_ref), (taps_hbm, taps_ref),
    )):
        inputs.append(pltpu.make_async_copy(src, dst, in_sem.at[i]))
        inputs[-1].start()

    is_early = me % ACROSS_Z < EARLY
    others = chans // ACROSS_Z * EARLY * 2
    n_early = others + 1 - 2 * is_early.astype(jnp.int32)
    n_late = 2 * chans - others - 2 + 2 * is_early.astype(jnp.int32) + n_rows - 1
    barrier = pltpu.get_barrier_semaphore()
    counter = 2 * my_y + 1 - is_early.astype(jnp.int32)
    for chip in chips[::-1]:

        @pl.when(chip != me)
        def _(chip=chip):
            pl.semaphore_signal(barrier, inc=1, device_id=(chip, counter), device_id_type=MESH)

    for i in range(1, n_rows // 2):
        there = (my_y + i) % (n_rows // 2)
        pl.semaphore_signal(barrier, inc=1, device_id=(me, 2 * there + 1), device_id_type=MESH)
    pl.semaphore_signal(barrier, inc=1, device_id=(me, slab + 1 - 2 * core), device_id_type=MESH)

    inputs[0].wait()
    inputs[1].wait()
    col = col_ref[...].astype(F32)
    owner = iota((2 * half, 128), 0)
    owner = jnp.where(owner < half, 2 * owner, 2 * (owner - half) + 1)
    first = (owner * width - (SUPPORT - 1 - CENTRE)).astype(F32)
    reach = []
    for n, (c, h) in enumerate(pieces):
        at = col[c : c + 1, h * 128 : h * 128 + 128] - first
        inside = (at >= 0.0) & (at <= float(width + SUPPORT - 2))
        hit = jnp.where(inside, 1.0, 0.0)
        reach.append(hit)
        e_ref[n * 2 * half : (n + 1) * 2 * half, :] = hit.astype(BF16)
        at = jnp.where(inside, at, 0.0).astype(BF16)
        for par in range(2):
            a_ref[par, 13 * half : 14 * half, n * 128 : n * 128 + 128] = at[par * half : (par + 1) * half]
    before = jnp.where(iota((128, 256), 0) < iota((128, 256), 1), 1.0, 0.0).astype(BF16)
    counts = matmul(e_ref[...], before)
    fullest = counts[: 2 * half, 128:]
    for n in range(1, len(pieces)):
        fullest = fullest + counts[n * 2 * half : (n + 1) * 2 * half, 128:]
    inputs[2].wait()
    inputs[3].wait()
    weight = weight_ref[...]
    weight_sum = jnp.sum(weight, axis=1, keepdims=True)
    on_diagonal = iota((n_chan, n_chan), 0) == iota((n_chan, n_chan), 1)
    taylor = [
        jnp.sum(jnp.where(on_diagonal, taylor_ref[t : t + 1, :], 0.0), axis=1, keepdims=True) for t in range(TERMS)
    ]
    lane = iota((1, 128), 1)
    part = jnp.where(lane == len(PAIRS), jnp.max(fullest, axis=0, keepdims=True), 0.0)
    for i, (a, b) in enumerate(PAIRS):
        entry = jnp.sum(taylor[a] * taylor[b] * weight_sum, axis=0, keepdims=True)
        part = jnp.where(lane == i, entry, part)
    hess_mine[...] = part
    hess_chan[pl.ds(me, 1)] = part[None]

    def gather(values):
        return jnp.where(lane == len(PAIRS), jnp.max(values, axis=0), jnp.sum(values, axis=0))

    def part_with(partner, sender):
        return pltpu.make_async_remote_copy(
            src_ref=hess_mine, dst_ref=hess_chan.at[sender], send_sem=hess_send, recv_sem=hess_recv,
            device_id=(partner, slab), device_id_type=MESH,
        )

    all_parts = pltpu.make_async_remote_copy(
        src_ref=hess_chan.at[pl.ds(0, chans - 1)], dst_ref=hess_chan.at[pl.ds(0, chans - 1)],
        send_sem=hess_send, recv_sem=hess_recv, device_id=(me, slab), device_id_type=MESH,
    )

    def to_chips(early, start):
        for chip in chips:
            if (chip % ACROSS_Z < EARLY) == early:

                @pl.when(chip != me)
                def _(chip=chip):
                    start(chip)

    @pl.when(core == 0)
    def _():
        pl.semaphore_wait(barrier, n_early)
        pl.semaphore_signal(early_here, inc=1, device_id=(me, slab + 1), device_id_type=MESH)

    @pl.when(core == 1)
    def _():
        pl.semaphore_wait(early_here, 1)

    to_chips(True, lambda chip: part_with(chip, me).start())

    start = jnp.zeros((2 * half, 128), F32)
    base = (round_ref[0] * SLOTS).astype(F32)
    slot = iota((SLOTS, 128), 0).astype(F32)
    for n in range(len(pieces)):
        now = counts[n * 2 * half : (n + 1) * 2 * half]
        rank = reach[n] * (now[:, :128] + start)
        start = start + now[:, 128:]
        for par in range(2):
            which = jnp.sum(rank[par * half : (par + 1) * half], axis=0, keepdims=True) - base
            b_ref[par, :, n * 128 : n * 128 + 128] = jnp.where(slot == which, 1.0, 0.0).astype(BF16)

    inputs[4].wait()
    inputs[5].wait()
    inputs[6].wait()
    scaled = []
    for t in range(TERMS):
        for p in range(2):
            scaled.append(taylor[t] * (weight * vis_ref[:, p, :]))
    rows = [two_parts(value) for value in scaled]
    rows = [high for high, _ in rows] + [low for _, low in rows] + [row_ref[...].astype(F32).astype(BF16)]
    rows = [value.astype(F32) for value in rows]
    for n, (c, h) in enumerate(pieces):
        hit = reach[n].astype(BF16)
        for i, value in enumerate(rows):
            spread = jnp.broadcast_to(value[c : c + 1, h * 128 : h * 128 + 128], (half, 128)).astype(BF16)
            for par in range(2):
                a_ref[par, i * half : (i + 1) * half, n * 128 : n * 128 + 128] = (
                    hit[par * half : (par + 1) * half] * spread
                )
    for par in range(2):
        tile = matmul_nt(a_ref[par], b_ref[par])
        for i in range(8):
            if i < 6:
                value = tile[i * half : (i + 1) * half] + tile[(6 + i) * half : (7 + i) * half]
            else:
                value = tile[(6 + i) * half : (7 + i) * half]
            mine[pl.ds(par * half * 8 + i, half, stride=8), :] = value

    def tile_to(owner):
        return pltpu.make_async_remote_copy(
            src_ref=mine.at[pl.ds(place(owner) * 8, 8)], dst_ref=theirs.at[me],
            send_sem=send_sem, recv_sem=recv_sem.at[me],
            device_id=(owner, slab), device_id_type=MESH,
        )

    def tile_from(sender):
        return pltpu.make_async_remote_copy(
            src_ref=mine.at[pl.ds(0, 8)], dst_ref=theirs.at[sender],
            send_sem=send_sem, recv_sem=recv_sem.at[sender],
            device_id=(sender, slab), device_id_type=MESH,
        )

    to_chips(True, lambda chip: tile_to(chip).start())

    @pl.when(core == 1)
    def _():
        pl.semaphore_wait(barrier, n_late)
        pl.semaphore_signal(late_here, inc=1, device_id=(me, slab - 1), device_id_type=MESH)

    @pl.when(core == 0)
    def _():
        pl.semaphore_wait(late_here, 1)

    to_chips(False, lambda chip: part_with(chip, me).start())
    to_chips(False, lambda chip: tile_to(chip).start())
    theirs[me] = mine[pl.ds(pl.multiple_of(place(me) * 8, 8), 8), :]

    tap_of = iota((ROWS_DEV, ROWS_DEV), 1) - iota((ROWS_DEV, ROWS_DEV), 0) + CENTRE
    row_taps = jnp.zeros((ROWS_DEV, ROWS_DEV), F32)
    for k in range(SUPPORT):
        row_taps = jnp.where(tap_of == k, taps_ref[k], row_taps)
    row_high, row_low = two_parts(row_taps)

    half_cell = iota((HALF, 128), 0).astype(F32)
    row_cell = iota((2 * ROWS_DEV, 128), 0).astype(F32)
    def arrived(g):
        for chip in chips[g : g + PER_STEP]:

            @pl.when(chip != me)
            def _(chip=chip):
                tile_from(chip).wait_recv()

    def grid_step(g):
        a_parts, b_parts = [], []
        for i in chips[g : g + PER_STEP]:
            tile = theirs[i]
            high = tile.astype(BF16).astype(F32)
            low = tile - high
            at = tile[7:8]
            halves = jnp.floor(at * 0.5)
            key = tile[6:7] + (at - 2.0 * halves) * float(ROWS_DEV)
            b_parts.append(jnp.where(row_cell == key, 1.0, 0.0).astype(BF16))
            here = half_cell == halves
            a_parts.append(
                jnp.concatenate(
                    [jnp.where(here, part_of[v : v + 1], 0.0).astype(BF16) for part_of in (high, low) for v in range(6)],
                    axis=0,
                )
            )
        total = matmul_nt(jnp.concatenate(a_parts, axis=1), jnp.concatenate(b_parts, axis=1))
        if g == 0:
            cells[...] = total
        else:
            cells[...] += total

    all_parts.wait_recv()
    chan_sum = gather(hess_chan[...])
    hess_sum[...] = chan_sum
    hess_rows[pl.ds(slab, 1)] = chan_sum[None]
    row_copies = []
    for i in range(1, n_rows):
        copy = pltpu.make_async_remote_copy(
            src_ref=hess_sum, dst_ref=hess_rows.at[slab], send_sem=row_send.at[i], recv_sem=row_recv.at[i],
            device_id=(me, (slab + i) % n_rows), device_id_type=MESH,
        )
        copy.start()
        row_copies.append(copy)

    for g in range(0, chans, PER_STEP):
        arrived(g)
        grid_step(g)

    for par in range(2):
        x = cells[: 6 * HALF, par * 128 : par * 128 + 128] + cells[6 * HALF :, par * 128 : par * 128 + 128]
        high, low = two_parts(x)
        mixed[par * 6 * HALF : (par + 1) * 6 * HALF, :] = (
            matmul(high, row_high) + matmul(low, row_high) + matmul(high, row_low)
        )

    wide = width // 2
    col_taps = [jnp.full((8, 128), taps_ref[j], F32).astype(BF16).astype(F32)[:1] for j in range(SUPPORT)]
    for e in range(2):
        for tp in range(2 * TERMS):
            grid = jnp.zeros((wide, 128), F32)
            for j in range(SUPPORT):
                shift = e + SUPPORT - 1 - j
                at = ((shift % 2) * 6 + tp) * HALF + shift // 2
                grid = grid + col_taps[j] * mixed[at : at + wide, :]
            grids[e, tp] = grid

    all_parts.wait_send()
    pltpu.make_async_remote_copy(
        src_ref=theirs.at[pl.ds(0, chans - 1)], dst_ref=theirs.at[pl.ds(0, chans - 1)],
        send_sem=send_sem, recv_sem=recv_sem.at[0], device_id=(me, slab), device_id_type=MESH,
    ).wait_send()

    for copy in row_copies:
        copy.wait()
    hess = gather(hess_rows[...])
    entries = {}
    for i, (a, b) in enumerate(PAIRS):
        entries[a, b] = entries[b, a] = jnp.sum(jnp.where(lane == i, hess, 0.0), axis=1, keepdims=True)
    scale = entries[0, 0]
    m = [[entries[a, b] / scale for b in range(3)] for a in range(3)]

    def cross(u, v):
        return [u[1] * v[2] - u[2] * v[1], u[2] * v[0] - u[0] * v[2], u[0] * v[1] - u[1] * v[0]]

    across = [cross(m[1], m[2]), cross(m[2], m[0]), cross(m[0], m[1])]
    det = m[0][0] * across[0][0] + m[0][1] * across[0][1] + m[0][2] * across[0][2]
    inverse = [[across[b][a] / det for b in range(3)] for a in range(3)]
    count = jnp.max(jnp.where(lane == len(PAIRS), hess, 0.0))
    rounds_ref[0] = (count.astype(jnp.int32) + (SLOTS - 1)) // SLOTS

    for e in range(2):
        for p in range(2):
            terms = [grids[e, 2 * t + p] for t in range(TERMS)]
            for a in range(TERMS):
                value = inverse[a][0] * terms[0] + inverse[a][1] * terms[1] + inverse[a][2] * terms[2]
                out_ref[pl.ds(e * 6 + a * 2 + p, wide, stride=12), :] = value


def grid_round(chans, n_rows, width, which, arrays):
    hbm = pl.BlockSpec(memory_space=HBM)
    n_vis = arrays[0].shape[0] * arrays[0].shape[1]
    out = jax.ShapeDtypeStruct((width * TERMS * 2, ROWS_DEV), F32)
    return pl.pallas_call(
        functools.partial(kernel, chans, n_rows, width),
        out_shape=(pltpu.VMEM(out.shape, F32), pltpu.SMEM((1,), jnp.int32)),
        in_specs=[hbm] * 7,
        out_specs=(pl.BlockSpec(memory_space=pltpu.VMEM), pl.BlockSpec(memory_space=pltpu.SMEM)),
        scratch_shapes=[
            pltpu.SMEM((1,), jnp.int32),
            *[pltpu.VMEM(a.shape, a.dtype) for a in arrays[:-1]],
            pltpu.SMEM(arrays[-1].shape, F32),
            pltpu.VMEM((chans * 8, 128), F32),
            pltpu.VMEM((chans, 8, 128), F32),
            pltpu.VMEM((2, 14 * chans // 2, n_vis), BF16),
            pltpu.VMEM((2, 128, n_vis), BF16),
            pltpu.VMEM((n_vis // 128 * chans, 128), BF16),
            pltpu.VMEM((12 * HALF, 2 * ROWS_DEV), F32),
            pltpu.VMEM((12 * HALF, ROWS_DEV), F32),
            pltpu.VMEM((2, 2 * TERMS, width // 2, ROWS_DEV), F32),
            pltpu.VMEM((1, 128), F32),
            pltpu.VMEM((chans, 1, 128), F32),
            pltpu.VMEM((1, 128), F32),
            pltpu.VMEM((n_rows, 1, 128), F32),
            pltpu.SemaphoreType.DMA((7,)),
            pltpu.SemaphoreType.REGULAR,
            pltpu.SemaphoreType.REGULAR,
            pltpu.SemaphoreType.DMA,
            pltpu.SemaphoreType.DMA((chans,)),
            pltpu.SemaphoreType.DMA((n_rows,)),
            pltpu.SemaphoreType.DMA((n_rows,)),
            pltpu.SemaphoreType.DMA,
            pltpu.SemaphoreType.DMA,
        ],
        compiler_params=pltpu.CompilerParams(
            collective_id=0, has_side_effects=True, vmem_limit_bytes=40 * 1024 * 1024
        ),
    )(*[pltpu.with_memory_space_constraint(a, HBM) for a in (which, *arrays)])


def body(row_cells, col_cells, visibilities, imaging_weights, taylor_weights, kernel_taps):
    arrays = (row_cells, col_cells, visibilities, imaging_weights, taylor_weights.T, kernel_taps)
    chans, n_rows = lax.axis_size("chan"), lax.axis_size("rows")
    width = NCOL // chans

    def more(state):
        return state[0] < state[1]

    def step(state):
        done, _, total = state
        part, rounds = grid_round(chans, n_rows, width, done[None], arrays)
        return done + 1, rounds[0], total + part

    part, rounds = grid_round(chans, n_rows, width, jnp.zeros((1,), jnp.int32), arrays)
    _, _, total = lax.while_loop(more, step, (jnp.int32(1), rounds[0], part))
    return total.reshape(width, TERMS, 2, ROWS_DEV)


def solution(mesh):
    in_specs = (
        P("chan", "rows"),
        P("chan", "rows"),
        P("chan", None, "rows"),
        P("chan", "rows"),
        P("chan", None),
        P(),
    )
    out_specs = P("chan", None, None, "rows")
    return jax.shard_map(body, mesh=mesh, in_specs=in_specs, out_specs=out_specs, check_vma=False)
```

```python
import functools

import jax
import jax.numpy as jnp
from jax import lax
from jax.experimental import pallas as pl
from jax.experimental.pallas import tpu as pltpu
from jax.sharding import PartitionSpec as P

NCOL = 2048
TERMS = 3
ROWS_DEV = 128
SUPPORT = 8
CENTRE = SUPPORT // 2
SLOTS = 128
PAIRS = ((0, 0), (0, 1), (0, 2), (1, 1), (1, 2), (2, 2))
ACROSS_X, ACROSS_Z = 4, 8
Z_ORDER = (0, 1, 2, 3, 5, 6, 4, 7)
LEAD = 1
EARLY = 3
HALF = 48
PER_STEP = 4

MESH = pl.DeviceIdType.MESH
F32 = jnp.float32
BF16 = jnp.bfloat16
HBM = pltpu.HBM


def in_order_of_start():
    return [x * ACROSS_Z + z for z in Z_ORDER for x in range(ACROSS_X)]


def matmul_nt(a, b):
    return lax.dot_general(a, b, (((1,), (1,)), ((), ())), preferred_element_type=F32)


def matmul(a, b):
    return lax.dot_general(a, b, (((1,), (0,)), ((), ())), preferred_element_type=F32)


def iota(shape, axis):
    return lax.broadcasted_iota(jnp.int32, shape, axis)


def two_parts(value):
    high = value.astype(BF16)
    return high, (value - high.astype(F32)).astype(BF16)


def kernel(
    chans, n_rows, width,
    round_hbm, row_hbm, col_hbm, vis_hbm, weight_hbm, taylor_hbm, taps_hbm,
    out_ref, rounds_ref,
    round_ref, row_ref, col_ref, vis_ref, weight_ref, taylor_ref, taps_ref,
    mine, theirs, a_ref, b_ref, e_ref, cells, mixed, grids, hess_mine, hess_chan, hess_sum, hess_rows, hess_lead,
    in_sem, early_here, late_here, send_sem, recv_sem, row_send, row_recv, hess_send, hess_recv, lead_send, lead_recv,
):
    me, slab = lax.axis_index("chan"), lax.axis_index("rows")
    my_y, core = slab // 2, slab % 2
    chips = in_order_of_start()
    half = chans // 2
    n_chan = row_ref.shape[0]
    pieces = [(c, h) for c in range(n_chan) for h in range(2)]

    def place(owner):
        return (owner % 2) * half + owner // 2

    inputs = []
    for i, (src, dst) in enumerate((
        (col_hbm, col_ref), (round_hbm, round_ref), (weight_hbm, weight_ref), (taylor_hbm, taylor_ref),
        (vis_hbm, vis_ref), (row_hbm, row_ref), (taps_hbm, taps_ref),
    )):
        inputs.append(pltpu.make_async_copy(src, dst, in_sem.at[i]))
        inputs[-1].start()

    is_early = me % ACROSS_Z < EARLY
    others = chans // ACROSS_Z * EARLY * 2
    n_early = others + 1 - 2 * is_early.astype(jnp.int32)
    n_late = 2 * chans - others - 2 + 2 * is_early.astype(jnp.int32) + n_rows - 1
    barrier = pltpu.get_barrier_semaphore()
    counter = 2 * my_y + 1 - is_early.astype(jnp.int32)
    is_lead = (me == 0) & (slab == LEAD)
    lead_told = my_y != LEAD // 2
    n_early = n_early + lead_told.astype(jnp.int32)
    for chip in chips[::-1]:

        @pl.when(chip != me)
        def _(chip=chip):
            pl.semaphore_signal(barrier, inc=1, device_id=(chip, counter), device_id_type=MESH)

    for i in range(1, n_rows // 2):
        there = (my_y + i) % (n_rows // 2)
        pl.semaphore_signal(barrier, inc=1, device_id=(me, 2 * there + 1), device_id_type=MESH)
    pl.semaphore_signal(barrier, inc=1, device_id=(me, slab + 1 - 2 * core), device_id_type=MESH)

    @pl.when(is_lead)
    def _():
        for i in range(1, n_rows // 2):
            there = (my_y + i) % (n_rows // 2)

            @pl.loop(0, chans)
            def _(k, there=there):
                pl.semaphore_signal(barrier, inc=1, device_id=(chans - 1 - k, 2 * there), device_id_type=MESH)

    inputs[0].wait()
    inputs[1].wait()
    col = col_ref[...].astype(F32)
    owner = iota((2 * half, 128), 0)
    owner = jnp.where(owner < half, 2 * owner, 2 * (owner - half) + 1)
    first = (owner * width - (SUPPORT - 1 - CENTRE)).astype(F32)
    reach = []
    for n, (c, h) in enumerate(pieces):
        at = col[c : c + 1, h * 128 : h * 128 + 128] - first
        inside = (at >= 0.0) & (at <= float(width + SUPPORT - 2))
        hit = jnp.where(inside, 1.0, 0.0)
        reach.append(hit)
        e_ref[n * 2 * half : (n + 1) * 2 * half, :] = hit.astype(BF16)
        at = jnp.where(inside, at, 0.0).astype(BF16)
        for par in range(2):
            a_ref[par, 13 * half : 14 * half, n * 128 : n * 128 + 128] = at[par * half : (par + 1) * half]
    before = jnp.where(iota((128, 256), 0) < iota((128, 256), 1), 1.0, 0.0).astype(BF16)
    counts = matmul(e_ref[...], before)
    fullest = counts[: 2 * half, 128:]
    for n in range(1, len(pieces)):
        fullest = fullest + counts[n * 2 * half : (n + 1) * 2 * half, 128:]
    inputs[2].wait()
    inputs[3].wait()
    weight = weight_ref[...]
    weight_sum = jnp.sum(weight, axis=1, keepdims=True)
    on_diagonal = iota((n_chan, n_chan), 0) == iota((n_chan, n_chan), 1)
    taylor = [
        jnp.sum(jnp.where(on_diagonal, taylor_ref[t : t + 1, :], 0.0), axis=1, keepdims=True) for t in range(TERMS)
    ]
    lane = iota((1, 128), 1)
    part = jnp.where(lane == len(PAIRS), jnp.max(fullest, axis=0, keepdims=True), 0.0)
    for i, (a, b) in enumerate(PAIRS):
        entry = jnp.sum(taylor[a] * taylor[b] * weight_sum, axis=0, keepdims=True)
        part = jnp.where(lane == i, entry, part)
    hess_mine[...] = part
    hess_chan[pl.ds(me, 1)] = part[None]

    def gather(values):
        return jnp.where(lane == len(PAIRS), jnp.max(values, axis=0), jnp.sum(values, axis=0))

    def part_with(partner, sender):
        return pltpu.make_async_remote_copy(
            src_ref=hess_mine, dst_ref=hess_chan.at[sender], send_sem=hess_send, recv_sem=hess_recv,
            device_id=(partner, slab), device_id_type=MESH,
        )

    all_parts = pltpu.make_async_remote_copy(
        src_ref=hess_chan.at[pl.ds(0, chans - 1)], dst_ref=hess_chan.at[pl.ds(0, chans - 1)],
        send_sem=hess_send, recv_sem=hess_recv, device_id=(me, slab), device_id_type=MESH,
    )

    def to_chips(early, start):
        for chip in chips:
            if (chip % ACROSS_Z < EARLY) == early:

                @pl.when(chip != me)
                def _(chip=chip):
                    start(chip)

    @pl.when(core == 0)
    def _():
        pl.semaphore_wait(barrier, n_early)
        pl.semaphore_signal(early_here, inc=1, device_id=(me, slab + 1), device_id_type=MESH)

    @pl.when(core == 1)
    def _():
        pl.semaphore_wait(early_here, 1)

    part_to_lead = pltpu.make_async_remote_copy(
        src_ref=hess_mine, dst_ref=hess_lead.at[slab, me], send_sem=lead_send, recv_sem=lead_recv,
        device_id=(0, LEAD), device_id_type=MESH,
    )

    @pl.when(slab != LEAD)
    def _():
        part_to_lead.start()

    to_chips(True, lambda chip: part_with(chip, me).start())

    start = jnp.zeros((2 * half, 128), F32)
    base = (round_ref[0] * SLOTS).astype(F32)
    slot = iota((SLOTS, 128), 0).astype(F32)
    for n in range(len(pieces)):
        now = counts[n * 2 * half : (n + 1) * 2 * half]
        rank = reach[n] * (now[:, :128] + start)
        start = start + now[:, 128:]
        for par in range(2):
            which = jnp.sum(rank[par * half : (par + 1) * half], axis=0, keepdims=True) - base
            b_ref[par, :, n * 128 : n * 128 + 128] = jnp.where(slot == which, 1.0, 0.0).astype(BF16)

    inputs[4].wait()
    inputs[5].wait()
    inputs[6].wait()
    scaled = []
    for t in range(TERMS):
        for p in range(2):
            scaled.append(taylor[t] * (weight * vis_ref[:, p, :]))
    rows = [two_parts(value) for value in scaled]
    rows = [high for high, _ in rows] + [low for _, low in rows] + [row_ref[...].astype(F32).astype(BF16)]
    rows = [value.astype(F32) for value in rows]
    for n, (c, h) in enumerate(pieces):
        hit = reach[n].astype(BF16)
        for i, value in enumerate(rows):
            spread = jnp.broadcast_to(value[c : c + 1, h * 128 : h * 128 + 128], (half, 128)).astype(BF16)
            for par in range(2):
                a_ref[par, i * half : (i + 1) * half, n * 128 : n * 128 + 128] = (
                    hit[par * half : (par + 1) * half] * spread
                )
    for par in range(2):
        tile = matmul_nt(a_ref[par], b_ref[par])
        for i in range(8):
            if i < 6:
                value = tile[i * half : (i + 1) * half] + tile[(6 + i) * half : (7 + i) * half]
            else:
                value = tile[(6 + i) * half : (7 + i) * half]
            mine[pl.ds(par * half * 8 + i, half, stride=8), :] = value

    def tile_to(owner):
        return pltpu.make_async_remote_copy(
            src_ref=mine.at[pl.ds(place(owner) * 8, 8)], dst_ref=theirs.at[me],
            send_sem=send_sem, recv_sem=recv_sem.at[me],
            device_id=(owner, slab), device_id_type=MESH,
        )

    def tile_from(sender):
        return pltpu.make_async_remote_copy(
            src_ref=mine.at[pl.ds(0, 8)], dst_ref=theirs.at[sender],
            send_sem=send_sem, recv_sem=recv_sem.at[sender],
            device_id=(sender, slab), device_id_type=MESH,
        )

    to_chips(True, lambda chip: tile_to(chip).start())

    @pl.when(core == 1)
    def _():
        pl.semaphore_wait(barrier, n_late)
        pl.semaphore_signal(late_here, inc=1, device_id=(me, slab - 1), device_id_type=MESH)

    @pl.when(core == 0)
    def _():
        pl.semaphore_wait(late_here, 1)

    to_chips(False, lambda chip: part_with(chip, me).start())
    to_chips(False, lambda chip: tile_to(chip).start())
    theirs[me] = mine[pl.ds(pl.multiple_of(place(me) * 8, 8), 8), :]

    tap_of = iota((ROWS_DEV, ROWS_DEV), 1) - iota((ROWS_DEV, ROWS_DEV), 0) + CENTRE
    row_taps = jnp.zeros((ROWS_DEV, ROWS_DEV), F32)
    for k in range(SUPPORT):
        row_taps = jnp.where(tap_of == k, taps_ref[k], row_taps)
    row_high, row_low = two_parts(row_taps)

    half_cell = iota((HALF, 128), 0).astype(F32)
    row_cell = iota((2 * ROWS_DEV, 128), 0).astype(F32)
    def arrived(g):
        for chip in chips[g : g + PER_STEP]:

            @pl.when(chip != me)
            def _(chip=chip):
                tile_from(chip).wait_recv()

    def grid_step(g):
        a_parts, b_parts = [], []
        for i in chips[g : g + PER_STEP]:
            tile = theirs[i]
            high = tile.astype(BF16).astype(F32)
            low = tile - high
            at = tile[7:8]
            halves = jnp.floor(at * 0.5)
            key = tile[6:7] + (at - 2.0 * halves) * float(ROWS_DEV)
            b_parts.append(jnp.where(row_cell == key, 1.0, 0.0).astype(BF16))
            here = half_cell == halves
            a_parts.append(
                jnp.concatenate(
                    [jnp.where(here, part_of[v : v + 1], 0.0).astype(BF16) for part_of in (high, low) for v in range(6)],
                    axis=0,
                )
            )
        total = matmul_nt(jnp.concatenate(a_parts, axis=1), jnp.concatenate(b_parts, axis=1))
        if g == 0:
            cells[...] = total
        else:
            cells[...] += total

    all_parts.wait_recv()
    chan_sum = gather(hess_chan[...])
    hess_sum[...] = chan_sum
    hess_rows[pl.ds(slab, 1)] = chan_sum[None]
    def row_copy(i):
        return pltpu.make_async_remote_copy(
            src_ref=hess_sum, dst_ref=hess_rows.at[slab], send_sem=row_send.at[i], recv_sem=row_recv.at[i],
            device_id=(me, (slab + i) % n_rows), device_id_type=MESH,
        )

    def to_row(use):
        for i in range(1, n_rows):

            @pl.when((me != 0) | ((slab + i) % n_rows != LEAD))
            def _(i=i):
                use(row_copy(i))

    to_row(lambda copy: copy.start())

    for g in range(0, chans, PER_STEP):
        arrived(g)
        grid_step(g)

    for par in range(2):
        x = cells[: 6 * HALF, par * 128 : par * 128 + 128] + cells[6 * HALF :, par * 128 : par * 128 + 128]
        high, low = two_parts(x)
        mixed[par * 6 * HALF : (par + 1) * 6 * HALF, :] = (
            matmul(high, row_high) + matmul(low, row_high) + matmul(high, row_low)
        )

    wide = width // 2
    col_taps = [jnp.full((8, 128), taps_ref[j], F32).astype(BF16).astype(F32)[:1] for j in range(SUPPORT)]
    for e in range(2):
        for tp in range(2 * TERMS):
            grid = jnp.zeros((wide, 128), F32)
            for j in range(SUPPORT):
                shift = e + SUPPORT - 1 - j
                at = ((shift % 2) * 6 + tp) * HALF + shift // 2
                grid = grid + col_taps[j] * mixed[at : at + wide, :]
            grids[e, tp] = grid

    all_parts.wait_send()
    pltpu.make_async_remote_copy(
        src_ref=theirs.at[pl.ds(0, chans - 1)], dst_ref=theirs.at[pl.ds(0, chans - 1)],
        send_sem=send_sem, recv_sem=recv_sem.at[0], device_id=(me, slab), device_id_type=MESH,
    ).wait_send()

    to_row(lambda copy: copy.wait_send())

    @pl.when(slab != LEAD)
    def _():
        part_to_lead.wait_send()

    @pl.when(is_lead)
    def _():
        pltpu.make_async_remote_copy(
            src_ref=hess_lead.at[pl.ds(0, n_rows - 1)], dst_ref=hess_lead.at[pl.ds(0, n_rows - 1)],
            send_sem=lead_send, recv_sem=lead_recv, device_id=(me, slab), device_id_type=MESH,
        ).wait_recv()
        total = [gather(hess_lead[r]) for r in range(n_rows) if r != LEAD] + [hess_sum[...]]
        hess_mine[...] = gather(jnp.stack(total))

    @pl.when(jnp.logical_not(is_lead))
    def _():
        for i in range(1, n_rows):
            row_copy(i).wait_recv()
        hess_mine[...] = gather(hess_rows[...])

    hess = hess_mine[...]
    entries = {}
    for i, (a, b) in enumerate(PAIRS):
        entries[a, b] = entries[b, a] = jnp.sum(jnp.where(lane == i, hess, 0.0), axis=1, keepdims=True)
    scale = entries[0, 0]
    m = [[entries[a, b] / scale for b in range(3)] for a in range(3)]

    def cross(u, v):
        return [u[1] * v[2] - u[2] * v[1], u[2] * v[0] - u[0] * v[2], u[0] * v[1] - u[1] * v[0]]

    across = [cross(m[1], m[2]), cross(m[2], m[0]), cross(m[0], m[1])]
    det = m[0][0] * across[0][0] + m[0][1] * across[0][1] + m[0][2] * across[0][2]
    inverse = [[across[b][a] / det for b in range(3)] for a in range(3)]
    count = jnp.max(jnp.where(lane == len(PAIRS), hess, 0.0))
    rounds_ref[0] = (count.astype(jnp.int32) + (SLOTS - 1)) // SLOTS

    for e in range(2):
        for p in range(2):
            terms = [grids[e, 2 * t + p] for t in range(TERMS)]
            for a in range(TERMS):
                value = inverse[a][0] * terms[0] + inverse[a][1] * terms[1] + inverse[a][2] * terms[2]
                out_ref[pl.ds(e * 6 + a * 2 + p, wide, stride=12), :] = value


def grid_round(chans, n_rows, width, which, arrays):
    hbm = pl.BlockSpec(memory_space=HBM)
    n_vis = arrays[0].shape[0] * arrays[0].shape[1]
    out = jax.ShapeDtypeStruct((width * TERMS * 2, ROWS_DEV), F32)
    return pl.pallas_call(
        functools.partial(kernel, chans, n_rows, width),
        out_shape=(pltpu.VMEM(out.shape, F32), pltpu.SMEM((1,), jnp.int32)),
        in_specs=[hbm] * 7,
        out_specs=(pl.BlockSpec(memory_space=pltpu.VMEM), pl.BlockSpec(memory_space=pltpu.SMEM)),
        scratch_shapes=[
            pltpu.SMEM((1,), jnp.int32),
            *[pltpu.VMEM(a.shape, a.dtype) for a in arrays[:-1]],
            pltpu.SMEM(arrays[-1].shape, F32),
            pltpu.VMEM((chans * 8, 128), F32),
            pltpu.VMEM((chans, 8, 128), F32),
            pltpu.VMEM((2, 14 * chans // 2, n_vis), BF16),
            pltpu.VMEM((2, 128, n_vis), BF16),
            pltpu.VMEM((n_vis // 128 * chans, 128), BF16),
            pltpu.VMEM((12 * HALF, 2 * ROWS_DEV), F32),
            pltpu.VMEM((12 * HALF, ROWS_DEV), F32),
            pltpu.VMEM((2, 2 * TERMS, width // 2, ROWS_DEV), F32),
            pltpu.VMEM((1, 128), F32),
            pltpu.VMEM((chans, 1, 128), F32),
            pltpu.VMEM((1, 128), F32),
            pltpu.VMEM((n_rows, 1, 128), F32),
            pltpu.VMEM((n_rows, chans, 1, 128), F32),
            pltpu.SemaphoreType.DMA((7,)),
            pltpu.SemaphoreType.REGULAR,
            pltpu.SemaphoreType.REGULAR,
            pltpu.SemaphoreType.DMA,
            pltpu.SemaphoreType.DMA((chans,)),
            pltpu.SemaphoreType.DMA((n_rows,)),
            pltpu.SemaphoreType.DMA((n_rows,)),
            pltpu.SemaphoreType.DMA,
            pltpu.SemaphoreType.DMA,
            pltpu.SemaphoreType.DMA,
            pltpu.SemaphoreType.DMA,
        ],
        compiler_params=pltpu.CompilerParams(
            collective_id=0, has_side_effects=True, vmem_limit_bytes=40 * 1024 * 1024
        ),
    )(*[pltpu.with_memory_space_constraint(a, HBM) for a in (which, *arrays)])


def body(row_cells, col_cells, visibilities, imaging_weights, taylor_weights, kernel_taps):
    arrays = (row_cells, col_cells, visibilities, imaging_weights, taylor_weights.T, kernel_taps)
    chans, n_rows = lax.axis_size("chan"), lax.axis_size("rows")
    width = NCOL // chans

    def more(state):
        return state[0] < state[1]

    def step(state):
        done, _, total = state
        part, rounds = grid_round(chans, n_rows, width, done[None], arrays)
        return done + 1, rounds[0], total + part

    part, rounds = grid_round(chans, n_rows, width, jnp.zeros((1,), jnp.int32), arrays)
    _, _, total = lax.while_loop(more, step, (jnp.int32(1), rounds[0], part))
    return total.reshape(width, TERMS, 2, ROWS_DEV)


def solution(mesh):
    in_specs = (
        P("chan", "rows"),
        P("chan", "rows"),
        P("chan", None, "rows"),
        P("chan", "rows"),
        P("chan", None),
        P(),
    )
    out_specs = P("chan", None, None, "rows")
    return jax.shard_map(body, mesh=mesh, in_specs=in_specs, out_specs=out_specs, check_vma=False)
```

```python
import functools

import jax
import jax.numpy as jnp
from jax import lax
from jax.experimental import pallas as pl
from jax.experimental.pallas import tpu as pltpu
from jax.sharding import PartitionSpec as P

NCOL = 2048
TERMS = 3
ROWS_DEV = 128
SUPPORT = 8
CENTRE = SUPPORT // 2
SLOTS = 128
PAIRS = ((0, 0), (0, 1), (0, 2), (1, 1), (1, 2), (2, 2))
ACROSS_X, ACROSS_Z = 4, 8
Z_ORDER = (0, 1, 2, 5, 6, 7, 3, 4)
LEAD = 1
EARLY = 3
HALF = 40
PER_STEP = 4

MESH = pl.DeviceIdType.MESH
F32 = jnp.float32
BF16 = jnp.bfloat16
HBM = pltpu.HBM


def in_order_of_start():
    early = [x * ACROSS_Z + z for z in Z_ORDER[:EARLY] for x in range(ACROSS_X)]
    return early + [x * ACROSS_Z + z for x in range(ACROSS_X) for z in Z_ORDER[EARLY:]]


def matmul_nt(a, b):
    return lax.dot_general(a, b, (((1,), (1,)), ((), ())), preferred_element_type=F32)


def matmul(a, b):
    return lax.dot_general(a, b, (((1,), (0,)), ((), ())), preferred_element_type=F32)


def iota(shape, axis):
    return lax.broadcasted_iota(jnp.int32, shape, axis)


def two_parts(value):
    high = value.astype(BF16)
    return high, (value - high.astype(F32)).astype(BF16)


def kernel(
    chans, n_rows, width,
    round_hbm, row_hbm, col_hbm, vis_hbm, weight_hbm, taylor_hbm, taps_hbm,
    out_ref, rounds_ref,
    round_ref, row_ref, col_ref, vis_ref, weight_ref, taylor_ref, taps_ref,
    mine, theirs, a_ref, b_ref, e_ref, cells, mixed, grids, hess_mine, hess_chan, hess_sum, hess_rows, hess_lead,
    in_sem, early_here, late_here, send_sem, recv_sem, row_send, row_recv, hess_send, hess_recv, lead_send, lead_recv,
):
    me, slab = lax.axis_index("chan"), lax.axis_index("rows")
    my_y, core = slab // 2, slab % 2
    chips = in_order_of_start()
    half = chans // 2
    n_chan = row_ref.shape[0]
    pieces = [(c, h) for c in range(n_chan) for h in range(2)]

    def place(owner):
        return (owner % 2) * half + owner // 2

    inputs = []
    for i, (src, dst) in enumerate((
        (col_hbm, col_ref), (round_hbm, round_ref), (weight_hbm, weight_ref), (taylor_hbm, taylor_ref),
        (vis_hbm, vis_ref), (row_hbm, row_ref), (taps_hbm, taps_ref),
    )):
        inputs.append(pltpu.make_async_copy(src, dst, in_sem.at[i]))
        inputs[-1].start()

    is_early = me % ACROSS_Z < EARLY
    others = chans // ACROSS_Z * EARLY * 2
    n_early = others + 1 - 2 * is_early.astype(jnp.int32)
    n_late = 2 * chans - others - 2 + 2 * is_early.astype(jnp.int32) + n_rows - 1
    barrier = pltpu.get_barrier_semaphore()
    counter = 2 * my_y + 1 - is_early.astype(jnp.int32)
    is_lead = (me == 0) & (slab == LEAD)
    lead_told = my_y != LEAD // 2
    n_early = n_early + lead_told.astype(jnp.int32)
    for chip in chips:

        @pl.when(chip != me)
        def _(chip=chip):
            pl.semaphore_signal(barrier, inc=1, device_id=(chip, counter), device_id_type=MESH)

    for i in range(1, n_rows // 2):
        there = (my_y + i) % (n_rows // 2)
        pl.semaphore_signal(barrier, inc=1, device_id=(me, 2 * there + 1), device_id_type=MESH)
    pl.semaphore_signal(barrier, inc=1, device_id=(me, slab + 1 - 2 * core), device_id_type=MESH)

    @pl.when(is_lead)
    def _():
        for i in range(1, n_rows // 2):
            there = (my_y + i) % (n_rows // 2)

            @pl.loop(0, chans)
            def _(k, there=there):
                pl.semaphore_signal(barrier, inc=1, device_id=(chans - 1 - k, 2 * there), device_id_type=MESH)

    inputs[0].wait()
    inputs[1].wait()
    col = col_ref[...].astype(F32)
    owner = iota((2 * half, 128), 0)
    owner = jnp.where(owner < half, 2 * owner, 2 * (owner - half) + 1)
    first = (owner * width - (SUPPORT - 1 - CENTRE)).astype(F32)
    reach = []
    for n, (c, h) in enumerate(pieces):
        at = col[c : c + 1, h * 128 : h * 128 + 128] - first
        inside = (at >= 0.0) & (at <= float(width + SUPPORT - 2))
        hit = jnp.where(inside, 1.0, 0.0)
        reach.append(hit)
        e_ref[n * 2 * half : (n + 1) * 2 * half, :] = hit.astype(BF16)
        at = jnp.where(inside, at, 0.0).astype(BF16)
        for par in range(2):
            a_ref[par, 13 * half : 14 * half, n * 128 : n * 128 + 128] = at[par * half : (par + 1) * half]
    before = jnp.where(iota((128, 256), 0) < iota((128, 256), 1), 1.0, 0.0).astype(BF16)
    counts = matmul(e_ref[...], before)
    fullest = counts[: 2 * half, 128:]
    for n in range(1, len(pieces)):
        fullest = fullest + counts[n * 2 * half : (n + 1) * 2 * half, 128:]
    inputs[2].wait()
    inputs[3].wait()
    weight = weight_ref[...]
    weight_sum = jnp.sum(weight, axis=1, keepdims=True)
    on_diagonal = iota((n_chan, n_chan), 0) == iota((n_chan, n_chan), 1)
    taylor = [
        jnp.sum(jnp.where(on_diagonal, taylor_ref[t : t + 1, :], 0.0), axis=1, keepdims=True) for t in range(TERMS)
    ]
    lane = iota((1, 128), 1)
    part = jnp.where(lane == len(PAIRS), jnp.max(fullest, axis=0, keepdims=True), 0.0)
    for i, (a, b) in enumerate(PAIRS):
        entry = jnp.sum(taylor[a] * taylor[b] * weight_sum, axis=0, keepdims=True)
        part = jnp.where(lane == i, entry, part)
    hess_mine[...] = part
    hess_chan[pl.ds(me, 1)] = part[None]

    def gather(values):
        return jnp.where(lane == len(PAIRS), jnp.max(values, axis=0), jnp.sum(values, axis=0))

    def part_with(partner, sender):
        return pltpu.make_async_remote_copy(
            src_ref=hess_mine, dst_ref=hess_chan.at[sender], send_sem=hess_send, recv_sem=hess_recv,
            device_id=(partner, slab), device_id_type=MESH,
        )

    all_parts = pltpu.make_async_remote_copy(
        src_ref=hess_chan.at[pl.ds(0, chans - 1)], dst_ref=hess_chan.at[pl.ds(0, chans - 1)],
        send_sem=hess_send, recv_sem=hess_recv, device_id=(me, slab), device_id_type=MESH,
    )

    def to_chips(early, start):
        for chip in chips:
            if (chip % ACROSS_Z < EARLY) == early:

                @pl.when(chip != me)
                def _(chip=chip):
                    start(chip)

    @pl.when(core == 0)
    def _():
        pl.semaphore_wait(barrier, n_early)
        pl.semaphore_signal(early_here, inc=1, device_id=(me, slab + 1), device_id_type=MESH)

    @pl.when(core == 1)
    def _():
        pl.semaphore_wait(early_here, 1)

    part_to_lead = pltpu.make_async_remote_copy(
        src_ref=hess_mine, dst_ref=hess_lead.at[slab, me], send_sem=lead_send, recv_sem=lead_recv,
        device_id=(0, LEAD), device_id_type=MESH,
    )

    @pl.when(slab != LEAD)
    def _():
        part_to_lead.start()

    to_chips(True, lambda chip: part_with(chip, me).start())

    start = jnp.zeros((2 * half, 128), F32)
    base = (round_ref[0] * SLOTS).astype(F32)
    slot = iota((SLOTS, 128), 0).astype(F32)
    for n in range(len(pieces)):
        now = counts[n * 2 * half : (n + 1) * 2 * half]
        rank = reach[n] * (now[:, :128] + start)
        start = start + now[:, 128:]
        for par in range(2):
            which = jnp.sum(rank[par * half : (par + 1) * half], axis=0, keepdims=True) - base
            b_ref[par, :, n * 128 : n * 128 + 128] = jnp.where(slot == which, 1.0, 0.0).astype(BF16)

    inputs[4].wait()
    inputs[5].wait()
    inputs[6].wait()
    scaled = []
    for t in range(TERMS):
        for p in range(2):
            scaled.append(taylor[t] * (weight * vis_ref[:, p, :]))
    rows = [two_parts(value) for value in scaled]
    rows = [high for high, _ in rows] + [low for _, low in rows] + [row_ref[...].astype(F32).astype(BF16)]
    rows = [value.astype(F32) for value in rows]
    for n, (c, h) in enumerate(pieces):
        hit = reach[n].astype(BF16)
        for i, value in enumerate(rows):
            spread = jnp.broadcast_to(value[c : c + 1, h * 128 : h * 128 + 128], (half, 128)).astype(BF16)
            for par in range(2):
                a_ref[par, i * half : (i + 1) * half, n * 128 : n * 128 + 128] = (
                    hit[par * half : (par + 1) * half] * spread
                )
    for par in range(2):
        tile = matmul_nt(a_ref[par], b_ref[par])
        for i in range(8):
            if i < 6:
                value = tile[i * half : (i + 1) * half] + tile[(6 + i) * half : (7 + i) * half]
            else:
                value = tile[(6 + i) * half : (7 + i) * half]
            mine[pl.ds(par * half * 8 + i, half, stride=8), :] = value

    def tile_to(owner):
        return pltpu.make_async_remote_copy(
            src_ref=mine.at[pl.ds(place(owner) * 8, 8)], dst_ref=theirs.at[me],
            send_sem=send_sem, recv_sem=recv_sem.at[me],
            device_id=(owner, slab), device_id_type=MESH,
        )

    def tile_from(sender):
        return pltpu.make_async_remote_copy(
            src_ref=mine.at[pl.ds(0, 8)], dst_ref=theirs.at[sender],
            send_sem=send_sem, recv_sem=recv_sem.at[sender],
            device_id=(sender, slab), device_id_type=MESH,
        )

    to_chips(True, lambda chip: tile_to(chip).start())

    @pl.when(core == 1)
    def _():
        pl.semaphore_wait(barrier, n_late)
        pl.semaphore_signal(late_here, inc=1, device_id=(me, slab - 1), device_id_type=MESH)

    @pl.when(core == 0)
    def _():
        pl.semaphore_wait(late_here, 1)

    to_chips(False, lambda chip: part_with(chip, me).start())
    to_chips(False, lambda chip: tile_to(chip).start())
    theirs[me] = mine[pl.ds(pl.multiple_of(place(me) * 8, 8), 8), :]

    tap_of = iota((ROWS_DEV, ROWS_DEV), 1) - iota((ROWS_DEV, ROWS_DEV), 0) + CENTRE
    row_taps = jnp.zeros((ROWS_DEV, ROWS_DEV), F32)
    for k in range(SUPPORT):
        row_taps = jnp.where(tap_of == k, taps_ref[k], row_taps)
    row_high, row_low = two_parts(row_taps)
    twice_high = jnp.concatenate([row_high, row_high], axis=0)

    half_cell = iota((HALF, 128), 0).astype(F32)
    row_cell = iota((2 * ROWS_DEV, 128), 0).astype(F32)
    def arrived(g):
        for chip in chips[g : g + PER_STEP]:

            @pl.when(chip != me)
            def _(chip=chip):
                tile_from(chip).wait_recv()

    def grid_step(g):
        a_parts, b_parts = [], []
        for i in chips[g : g + PER_STEP]:
            tile = theirs[i]
            high = tile.astype(BF16).astype(F32)
            low = tile - high
            at = tile[7:8]
            halves = jnp.floor(at * 0.5)
            key = tile[6:7] + (at - 2.0 * halves) * float(ROWS_DEV)
            b_parts.append(jnp.where(row_cell == key, 1.0, 0.0).astype(BF16))
            here = half_cell == halves
            a_parts.append(
                jnp.concatenate(
                    [jnp.where(here, part_of[v : v + 1], 0.0) for part_of in (high, low) for v in range(6)],
                    axis=0,
                ).astype(BF16)
            )
        total = matmul_nt(jnp.concatenate(a_parts, axis=1), jnp.concatenate(b_parts, axis=1))
        if g == 0:
            cells[...] = total
        else:
            cells[...] += total

    all_parts.wait_recv()
    chan_sum = gather(hess_chan[...])
    hess_sum[...] = chan_sum
    hess_rows[pl.ds(slab, 1)] = chan_sum[None]
    def row_copy(i):
        return pltpu.make_async_remote_copy(
            src_ref=hess_sum, dst_ref=hess_rows.at[slab], send_sem=row_send.at[i], recv_sem=row_recv.at[i],
            device_id=(me, (slab + i) % n_rows), device_id_type=MESH,
        )

    def to_row(use):
        for i in range(1, n_rows):

            @pl.when((me != 0) | ((slab + i) % n_rows != LEAD))
            def _(i=i):
                use(row_copy(i))

    to_row(lambda copy: copy.start())

    for g in range(0, chans, PER_STEP):
        arrived(g)
        grid_step(g)

    for par in range(2):
        x = cells[: 6 * HALF, par * 128 : par * 128 + 128] + cells[6 * HALF :, par * 128 : par * 128 + 128]
        high, low = two_parts(x)
        mixed[par * 6 * HALF : (par + 1) * 6 * HALF, :] = (
            matmul(jnp.concatenate([high, low], axis=1), twice_high) + matmul(high, row_low)
        )

    wide = width // 2
    col_taps = [jnp.full((8, 128), taps_ref[j], F32).astype(BF16).astype(F32)[:1] for j in range(SUPPORT)]
    for e in range(2):
        for tp in range(2 * TERMS):
            grid = jnp.zeros((wide, 128), F32)
            for j in range(SUPPORT):
                shift = e + SUPPORT - 1 - j
                at = ((shift % 2) * 6 + tp) * HALF + shift // 2
                grid = grid + col_taps[j] * mixed[at : at + wide, :]
            grids[e, tp] = grid

    all_parts.wait_send()
    pltpu.make_async_remote_copy(
        src_ref=theirs.at[pl.ds(0, chans - 1)], dst_ref=theirs.at[pl.ds(0, chans - 1)],
        send_sem=send_sem, recv_sem=recv_sem.at[0], device_id=(me, slab), device_id_type=MESH,
    ).wait_send()

    to_row(lambda copy: copy.wait_send())

    @pl.when(slab != LEAD)
    def _():
        part_to_lead.wait_send()

    @pl.when(is_lead)
    def _():
        pltpu.make_async_remote_copy(
            src_ref=hess_lead.at[pl.ds(0, n_rows - 1)], dst_ref=hess_lead.at[pl.ds(0, n_rows - 1)],
            send_sem=lead_send, recv_sem=lead_recv, device_id=(me, slab), device_id_type=MESH,
        ).wait_recv()
        total = [gather(hess_lead[r]) for r in range(n_rows) if r != LEAD] + [hess_sum[...]]
        hess_mine[...] = gather(jnp.stack(total))

    @pl.when(jnp.logical_not(is_lead))
    def _():
        for i in range(1, n_rows):
            row_copy(i).wait_recv()
        hess_mine[...] = gather(hess_rows[...])

    hess = hess_mine[...]
    entries = {}
    for i, (a, b) in enumerate(PAIRS):
        entries[a, b] = entries[b, a] = jnp.sum(jnp.where(lane == i, hess, 0.0), axis=1, keepdims=True)
    scale = entries[0, 0]
    m = [[entries[a, b] / scale for b in range(3)] for a in range(3)]

    def cross(u, v):
        return [u[1] * v[2] - u[2] * v[1], u[2] * v[0] - u[0] * v[2], u[0] * v[1] - u[1] * v[0]]

    across = [cross(m[1], m[2]), cross(m[2], m[0]), cross(m[0], m[1])]
    det = m[0][0] * across[0][0] + m[0][1] * across[0][1] + m[0][2] * across[0][2]
    inverse = [[across[b][a] / det for b in range(3)] for a in range(3)]
    count = jnp.max(jnp.where(lane == len(PAIRS), hess, 0.0))
    rounds_ref[0] = (count.astype(jnp.int32) + (SLOTS - 1)) // SLOTS

    for e in range(2):
        for p in range(2):
            terms = [grids[e, 2 * t + p] for t in range(TERMS)]
            for a in range(TERMS):
                value = inverse[a][0] * terms[0] + inverse[a][1] * terms[1] + inverse[a][2] * terms[2]
                out_ref[pl.ds(e * 6 + a * 2 + p, wide, stride=12), :] = value


def grid_round(chans, n_rows, width, which, arrays):
    hbm = pl.BlockSpec(memory_space=HBM)
    n_vis = arrays[0].shape[0] * arrays[0].shape[1]
    out = jax.ShapeDtypeStruct((width * TERMS * 2, ROWS_DEV), F32)
    return pl.pallas_call(
        functools.partial(kernel, chans, n_rows, width),
        out_shape=(pltpu.VMEM(out.shape, F32), pltpu.SMEM((1,), jnp.int32)),
        in_specs=[hbm] * 7,
        out_specs=(pl.BlockSpec(memory_space=pltpu.VMEM), pl.BlockSpec(memory_space=pltpu.SMEM)),
        scratch_shapes=[
            pltpu.SMEM((1,), jnp.int32),
            *[pltpu.VMEM(a.shape, a.dtype) for a in arrays[:-1]],
            pltpu.SMEM(arrays[-1].shape, F32),
            pltpu.VMEM((chans * 8, 128), F32),
            pltpu.VMEM((chans, 8, 128), F32),
            pltpu.VMEM((2, 14 * chans // 2, n_vis), BF16),
            pltpu.VMEM((2, 128, n_vis), BF16),
            pltpu.VMEM((n_vis // 128 * chans, 128), BF16),
            pltpu.VMEM((12 * HALF, 2 * ROWS_DEV), F32),
            pltpu.VMEM((12 * HALF, ROWS_DEV), F32),
            pltpu.VMEM((2, 2 * TERMS, width // 2, ROWS_DEV), F32),
            pltpu.VMEM((1, 128), F32),
            pltpu.VMEM((chans, 1, 128), F32),
            pltpu.VMEM((1, 128), F32),
            pltpu.VMEM((n_rows, 1, 128), F32),
            pltpu.VMEM((n_rows, chans, 1, 128), F32),
            pltpu.SemaphoreType.DMA((7,)),
            pltpu.SemaphoreType.REGULAR,
            pltpu.SemaphoreType.REGULAR,
            pltpu.SemaphoreType.DMA,
            pltpu.SemaphoreType.DMA((chans,)),
            pltpu.SemaphoreType.DMA((n_rows,)),
            pltpu.SemaphoreType.DMA((n_rows,)),
            pltpu.SemaphoreType.DMA,
            pltpu.SemaphoreType.DMA,
            pltpu.SemaphoreType.DMA,
            pltpu.SemaphoreType.DMA,
        ],
        compiler_params=pltpu.CompilerParams(
            collective_id=0, has_side_effects=True, vmem_limit_bytes=40 * 1024 * 1024
        ),
    )(*[pltpu.with_memory_space_constraint(a, HBM) for a in (which, *arrays)])


def body(row_cells, col_cells, visibilities, imaging_weights, taylor_weights, kernel_taps):
    arrays = (row_cells, col_cells, visibilities, imaging_weights, taylor_weights.T, kernel_taps)
    chans, n_rows = lax.axis_size("chan"), lax.axis_size("rows")
    width = NCOL // chans

    def more(state):
        return state[0] < state[1]

    def step(state):
        done, _, total = state
        part, rounds = grid_round(chans, n_rows, width, done[None], arrays)
        return done + 1, rounds[0], total + part

    part, rounds = grid_round(chans, n_rows, width, jnp.zeros((1,), jnp.int32), arrays)
    _, _, total = lax.while_loop(more, step, (jnp.int32(1), rounds[0], part))
    return total.reshape(width, TERMS, 2, ROWS_DEV)


def solution(mesh):
    in_specs = (
        P("chan", "rows"),
        P("chan", "rows"),
        P("chan", None, "rows"),
        P("chan", "rows"),
        P("chan", None),
        P(),
    )
    out_specs = P("chan", None, None, "rows")
    return jax.shard_map(body, mesh=mesh, in_specs=in_specs, out_specs=out_specs, check_vma=False)
```

```python
import functools

import jax
import jax.numpy as jnp
from jax import lax
from jax.experimental import pallas as pl
from jax.experimental.pallas import tpu as pltpu
from jax.sharding import PartitionSpec as P

NCOL = 2048
TERMS = 3
ROWS_DEV = 128
SUPPORT = 8
CENTRE = SUPPORT // 2
SLOTS = 128
PAIRS = ((0, 0), (0, 1), (0, 2), (1, 1), (1, 2), (2, 2))
ACROSS_X, ACROSS_Z = 4, 8
Z_ORDER = (0, 1, 2, 5, 6, 7, 3, 4)
LEAD = 1
EARLY = 3
HALF = 40
PER_STEP = 4

MESH = pl.DeviceIdType.MESH
F32 = jnp.float32
BF16 = jnp.bfloat16
HBM = pltpu.HBM


def in_order_of_start():
    early = [x * ACROSS_Z + z for z in Z_ORDER[:EARLY] for x in range(ACROSS_X)]
    return early + [x * ACROSS_Z + z for x in range(ACROSS_X) for z in Z_ORDER[EARLY:]]


def matmul_nt(a, b):
    return lax.dot_general(a, b, (((1,), (1,)), ((), ())), preferred_element_type=F32)


def matmul(a, b):
    return lax.dot_general(a, b, (((1,), (0,)), ((), ())), preferred_element_type=F32)


def iota(shape, axis):
    return lax.broadcasted_iota(jnp.int32, shape, axis)


def two_parts(value):
    high = value.astype(BF16)
    return high, (value - high.astype(F32)).astype(BF16)


def kernel(
    chans, n_rows, width,
    round_hbm, row_hbm, col_hbm, vis_hbm, weight_hbm, taylor_hbm, taps_hbm,
    out_ref, rounds_ref,
    round_ref, row_ref, col_ref, vis_ref, weight_ref, taylor_ref, taps_ref,
    mine, theirs, a_ref, b_ref, e_ref, cells, mixed, grids, hess_mine, hess_chan, hess_sum, hess_rows, hess_lead,
    in_sem, early_here, late_here, send_sem, recv_sem, row_send, row_recv, hess_send, hess_recv, lead_send, lead_recv,
):
    me, slab = lax.axis_index("chan"), lax.axis_index("rows")
    my_y, core = slab // 2, slab % 2
    chips = in_order_of_start()
    half = chans // 2
    n_chan = row_ref.shape[0]
    pieces = [(c, h) for c in range(n_chan) for h in range(2)]

    def place(owner):
        return (owner % 2) * half + owner // 2

    inputs = []
    for i, (src, dst) in enumerate((
        (col_hbm, col_ref), (round_hbm, round_ref), (weight_hbm, weight_ref), (taylor_hbm, taylor_ref),
        (vis_hbm, vis_ref), (row_hbm, row_ref), (taps_hbm, taps_ref),
    )):
        inputs.append(pltpu.make_async_copy(src, dst, in_sem.at[i]))
        inputs[-1].start()

    is_early = me % ACROSS_Z < EARLY
    others = chans // ACROSS_Z * EARLY * 2
    n_early = others + 1 - 2 * is_early.astype(jnp.int32)
    n_late = 2 * chans - others - 2 + 2 * is_early.astype(jnp.int32) + n_rows - 1
    barrier = pltpu.get_barrier_semaphore()
    counter = 2 * my_y + 1 - is_early.astype(jnp.int32)
    is_lead = (me == 0) & (slab == LEAD)
    lead_told = my_y != LEAD // 2
    n_early = n_early + lead_told.astype(jnp.int32)
    for chip in chips:

        @pl.when(chip != me)
        def _(chip=chip):
            pl.semaphore_signal(barrier, inc=1, device_id=(chip, counter), device_id_type=MESH)

    for i in range(1, n_rows // 2):
        there = (my_y + i) % (n_rows // 2)
        pl.semaphore_signal(barrier, inc=1, device_id=(me, 2 * there + 1), device_id_type=MESH)
    pl.semaphore_signal(barrier, inc=1, device_id=(me, slab + 1 - 2 * core), device_id_type=MESH)

    @pl.when(is_lead)
    def _():
        for i in range(1, n_rows // 2):
            there = (my_y + i) % (n_rows // 2)

            @pl.loop(0, chans)
            def _(k, there=there):
                pl.semaphore_signal(barrier, inc=1, device_id=(chans - 1 - k, 2 * there), device_id_type=MESH)

    inputs[0].wait()
    inputs[1].wait()
    col = col_ref[...].astype(F32)
    owner = iota((2 * half, 128), 0)
    owner = jnp.where(owner < half, 2 * owner, 2 * (owner - half) + 1)
    first = (owner * width - (SUPPORT - 1 - CENTRE)).astype(F32)
    reach = []
    for n, (c, h) in enumerate(pieces):
        at = col[c : c + 1, h * 128 : h * 128 + 128] - first
        inside = (at >= 0.0) & (at <= float(width + SUPPORT - 2))
        hit = jnp.where(inside, 1.0, 0.0)
        reach.append(hit)
        e_ref[n * 2 * half : (n + 1) * 2 * half, :] = hit.astype(BF16)
        at = jnp.where(inside, at, 0.0).astype(BF16)
        for par in range(2):
            a_ref[par, 13 * half : 14 * half, n * 128 : n * 128 + 128] = at[par * half : (par + 1) * half]
    before = jnp.where(iota((128, 256), 0) < iota((128, 256), 1), 1.0, 0.0).astype(BF16)
    counts = matmul(e_ref[...], before)
    fullest = counts[: 2 * half, 128:]
    for n in range(1, len(pieces)):
        fullest = fullest + counts[n * 2 * half : (n + 1) * 2 * half, 128:]
    inputs[2].wait()
    inputs[3].wait()
    weight = weight_ref[...]
    weight_sum = jnp.sum(weight, axis=1, keepdims=True)
    on_diagonal = iota((n_chan, n_chan), 0) == iota((n_chan, n_chan), 1)
    taylor = [
        jnp.sum(jnp.where(on_diagonal, taylor_ref[t : t + 1, :], 0.0), axis=1, keepdims=True) for t in range(TERMS)
    ]
    lane = iota((1, 128), 1)
    part = jnp.where(lane == len(PAIRS), jnp.max(fullest, axis=0, keepdims=True), 0.0)
    for i, (a, b) in enumerate(PAIRS):
        entry = jnp.sum(taylor[a] * taylor[b] * weight_sum, axis=0, keepdims=True)
        part = jnp.where(lane == i, entry, part)
    hess_mine[...] = part
    hess_chan[pl.ds(me, 1)] = part[None]

    def gather(values):
        return jnp.where(lane == len(PAIRS), jnp.max(values, axis=0), jnp.sum(values, axis=0))

    def part_with(partner, sender):
        return pltpu.make_async_remote_copy(
            src_ref=hess_mine, dst_ref=hess_chan.at[sender], send_sem=hess_send, recv_sem=hess_recv,
            device_id=(partner, slab), device_id_type=MESH,
        )

    all_parts = pltpu.make_async_remote_copy(
        src_ref=hess_chan.at[pl.ds(0, chans - 1)], dst_ref=hess_chan.at[pl.ds(0, chans - 1)],
        send_sem=hess_send, recv_sem=hess_recv, device_id=(me, slab), device_id_type=MESH,
    )

    def to_chips(early, start):
        for chip in chips:
            if (chip % ACROSS_Z < EARLY) == early:

                @pl.when(chip != me)
                def _(chip=chip):
                    start(chip)

    @pl.when(core == 0)
    def _():
        pl.semaphore_wait(barrier, n_early)
        pl.semaphore_signal(early_here, inc=1, device_id=(me, slab + 1), device_id_type=MESH)

    @pl.when(core == 1)
    def _():
        pl.semaphore_wait(early_here, 1)

    part_to_lead = pltpu.make_async_remote_copy(
        src_ref=hess_mine, dst_ref=hess_lead.at[slab, me], send_sem=lead_send, recv_sem=lead_recv,
        device_id=(0, LEAD), device_id_type=MESH,
    )

    @pl.when(slab != LEAD)
    def _():
        part_to_lead.start()

    to_chips(True, lambda chip: part_with(chip, me).start())

    start = jnp.zeros((2 * half, 128), F32)
    base = (round_ref[0] * SLOTS).astype(F32)
    slot = iota((SLOTS, 128), 0).astype(F32)
    for n in range(len(pieces)):
        now = counts[n * 2 * half : (n + 1) * 2 * half]
        rank = reach[n] * (now[:, :128] + start)
        start = start + now[:, 128:]
        for par in range(2):
            which = jnp.sum(rank[par * half : (par + 1) * half], axis=0, keepdims=True) - base
            b_ref[par, :, n * 128 : n * 128 + 128] = jnp.where(slot == which, 1.0, 0.0).astype(BF16)

    inputs[4].wait()
    inputs[5].wait()
    inputs[6].wait()
    scaled = []
    for t in range(TERMS):
        for p in range(2):
            scaled.append(taylor[t] * (weight * vis_ref[:, p, :]))
    rows = [two_parts(value) for value in scaled]
    rows = [high for high, _ in rows] + [low for _, low in rows] + [row_ref[...].astype(F32).astype(BF16)]
    rows = [value.astype(F32) for value in rows]
    for n, (c, h) in enumerate(pieces):
        hit = reach[n].astype(BF16)
        for i, value in enumerate(rows):
            spread = jnp.broadcast_to(value[c : c + 1, h * 128 : h * 128 + 128], (half, 128)).astype(BF16)
            for par in range(2):
                a_ref[par, i * half : (i + 1) * half, n * 128 : n * 128 + 128] = (
                    hit[par * half : (par + 1) * half] * spread
                )
    for par in range(2):
        tile = matmul_nt(a_ref[par], b_ref[par])
        for i in range(8):
            if i < 6:
                value = tile[i * half : (i + 1) * half] + tile[(6 + i) * half : (7 + i) * half]
            else:
                value = tile[(6 + i) * half : (7 + i) * half]
            mine[pl.ds(par * half * 8 + i, half, stride=8), :] = value

    def tile_to(owner):
        return pltpu.make_async_remote_copy(
            src_ref=mine.at[pl.ds(place(owner) * 8, 8)], dst_ref=theirs.at[me],
            send_sem=send_sem, recv_sem=recv_sem.at[me],
            device_id=(owner, slab), device_id_type=MESH,
        )

    def tile_from(sender):
        return pltpu.make_async_remote_copy(
            src_ref=mine.at[pl.ds(0, 8)], dst_ref=theirs.at[sender],
            send_sem=send_sem, recv_sem=recv_sem.at[sender],
            device_id=(sender, slab), device_id_type=MESH,
        )

    to_chips(True, lambda chip: tile_to(chip).start())

    @pl.when(core == 1)
    def _():
        pl.semaphore_wait(barrier, n_late)
        pl.semaphore_signal(late_here, inc=1, device_id=(me, slab - 1), device_id_type=MESH)

    @pl.when(core == 0)
    def _():
        pl.semaphore_wait(late_here, 1)

    to_chips(False, lambda chip: part_with(chip, me).start())
    to_chips(False, lambda chip: tile_to(chip).start())
    theirs[me] = mine[pl.ds(pl.multiple_of(place(me) * 8, 8), 8), :]

    tap_of = iota((ROWS_DEV, ROWS_DEV), 1) - iota((ROWS_DEV, ROWS_DEV), 0) + CENTRE
    row_taps = jnp.zeros((ROWS_DEV, ROWS_DEV), F32)
    for k in range(SUPPORT):
        row_taps = jnp.where(tap_of == k, taps_ref[k], row_taps)
    row_high, row_low = two_parts(row_taps)
    twice_high = jnp.concatenate([row_high, row_high], axis=0)

    half_cell = iota((HALF, 128), 0).astype(F32)
    row_cell = iota((2 * ROWS_DEV, 128), 0).astype(F32)
    def arrived(g):
        for chip in chips[g : g + PER_STEP]:

            @pl.when(chip != me)
            def _(chip=chip):
                tile_from(chip).wait_recv()

    def grid_step(g):
        a_parts, b_parts = [], []
        for i in chips[g : g + PER_STEP]:
            tile = theirs[i]
            high = tile.astype(BF16).astype(F32)
            low = tile - high
            at = tile[7:8]
            halves = jnp.floor(at * 0.5)
            key = tile[6:7] + (at - 2.0 * halves) * float(ROWS_DEV)
            b_parts.append(jnp.where(row_cell == key, 1.0, 0.0).astype(BF16))
            here = half_cell == halves
            a_parts.append(
                jnp.concatenate(
                    [jnp.where(here, part_of[v : v + 1], 0.0) for part_of in (high, low) for v in range(6)],
                    axis=0,
                ).astype(BF16)
            )
        total = matmul_nt(jnp.concatenate(a_parts, axis=1), jnp.concatenate(b_parts, axis=1))
        if g == 0:
            cells[...] = total
        else:
            cells[...] += total

    all_parts.wait_recv()
    chan_sum = gather(hess_chan[...])
    hess_sum[...] = chan_sum
    hess_rows[pl.ds(slab, 1)] = chan_sum[None]
    def row_copy(to, sender):
        return pltpu.make_async_remote_copy(
            src_ref=hess_sum, dst_ref=hess_rows.at[sender], send_sem=row_send.at[to], recv_sem=row_recv.at[sender],
            device_id=(me, to), device_id_type=MESH,
        )

    def to_row(use):
        for to in range(n_rows):

            @pl.when((slab != to) & (me != 0) if to == LEAD else slab != to)
            def _(to=to):
                use(row_copy(to, slab))

    to_row(lambda copy: copy.start())

    for g in range(0, chans, PER_STEP):
        arrived(g)
        grid_step(g)

    for par in range(2):
        x = cells[: 6 * HALF, par * 128 : par * 128 + 128] + cells[6 * HALF :, par * 128 : par * 128 + 128]
        high, low = two_parts(x)
        mixed[par * 6 * HALF : (par + 1) * 6 * HALF, :] = (
            matmul(jnp.concatenate([high, low], axis=1), twice_high) + matmul(high, row_low)
        )

    wide = width // 2
    col_taps = [jnp.full((8, 128), taps_ref[j], F32).astype(BF16).astype(F32)[:1] for j in range(SUPPORT)]
    for e in range(2):
        for tp in range(2 * TERMS):
            grid = jnp.zeros((wide, 128), F32)
            for j in range(SUPPORT):
                shift = e + SUPPORT - 1 - j
                at = ((shift % 2) * 6 + tp) * HALF + shift // 2
                grid = grid + col_taps[j] * mixed[at : at + wide, :]
            grids[e, tp] = grid

    all_parts.wait_send()
    pltpu.make_async_remote_copy(
        src_ref=theirs.at[pl.ds(0, chans - 1)], dst_ref=theirs.at[pl.ds(0, chans - 1)],
        send_sem=send_sem, recv_sem=recv_sem.at[0], device_id=(me, slab), device_id_type=MESH,
    ).wait_send()

    to_row(lambda copy: copy.wait_send())

    @pl.when(slab != LEAD)
    def _():
        part_to_lead.wait_send()

    @pl.when(is_lead)
    def _():
        pltpu.make_async_remote_copy(
            src_ref=hess_lead.at[pl.ds(0, n_rows - 1)], dst_ref=hess_lead.at[pl.ds(0, n_rows - 1)],
            send_sem=lead_send, recv_sem=lead_recv, device_id=(me, slab), device_id_type=MESH,
        ).wait_recv()
        total = [gather(hess_lead[r]) for r in range(n_rows) if r != LEAD] + [hess_sum[...]]
        hess_mine[...] = gather(jnp.stack(total))

    @pl.when(jnp.logical_not(is_lead))
    def _():
        for sender in range(n_rows):

            @pl.when(sender != slab)
            def _(sender=sender):
                row_copy(sender, sender).wait_recv()

        hess_mine[...] = gather(hess_rows[...])

    hess = hess_mine[...]
    entries = {}
    for i, (a, b) in enumerate(PAIRS):
        entries[a, b] = entries[b, a] = jnp.sum(jnp.where(lane == i, hess, 0.0), axis=1, keepdims=True)
    scale = entries[0, 0]
    m = [[entries[a, b] / scale for b in range(3)] for a in range(3)]

    def cross(u, v):
        return [u[1] * v[2] - u[2] * v[1], u[2] * v[0] - u[0] * v[2], u[0] * v[1] - u[1] * v[0]]

    across = [cross(m[1], m[2]), cross(m[2], m[0]), cross(m[0], m[1])]
    det = m[0][0] * across[0][0] + m[0][1] * across[0][1] + m[0][2] * across[0][2]
    inverse = [[across[b][a] / det for b in range(3)] for a in range(3)]
    count = jnp.max(jnp.where(lane == len(PAIRS), hess, 0.0))
    rounds_ref[0] = (count.astype(jnp.int32) + (SLOTS - 1)) // SLOTS

    for e in range(2):
        for p in range(2):
            terms = [grids[e, 2 * t + p] for t in range(TERMS)]
            for a in range(TERMS):
                value = inverse[a][0] * terms[0] + inverse[a][1] * terms[1] + inverse[a][2] * terms[2]
                out_ref[pl.ds(e * 6 + a * 2 + p, wide, stride=12), :] = value


def grid_round(chans, n_rows, width, which, arrays):
    hbm = pl.BlockSpec(memory_space=HBM)
    n_vis = arrays[0].shape[0] * arrays[0].shape[1]
    out = jax.ShapeDtypeStruct((width * TERMS * 2, ROWS_DEV), F32)
    return pl.pallas_call(
        functools.partial(kernel, chans, n_rows, width),
        out_shape=(pltpu.VMEM(out.shape, F32), pltpu.SMEM((1,), jnp.int32)),
        in_specs=[hbm] * 7,
        out_specs=(pl.BlockSpec(memory_space=pltpu.VMEM), pl.BlockSpec(memory_space=pltpu.SMEM)),
        scratch_shapes=[
            pltpu.SMEM((1,), jnp.int32),
            *[pltpu.VMEM(a.shape, a.dtype) for a in arrays[:-1]],
            pltpu.SMEM(arrays[-1].shape, F32),
            pltpu.VMEM((chans * 8, 128), F32),
            pltpu.VMEM((chans, 8, 128), F32),
            pltpu.VMEM((2, 14 * chans // 2, n_vis), BF16),
            pltpu.VMEM((2, 128, n_vis), BF16),
            pltpu.VMEM((n_vis // 128 * chans, 128), BF16),
            pltpu.VMEM((12 * HALF, 2 * ROWS_DEV), F32),
            pltpu.VMEM((12 * HALF, ROWS_DEV), F32),
            pltpu.VMEM((2, 2 * TERMS, width // 2, ROWS_DEV), F32),
            pltpu.VMEM((1, 128), F32),
            pltpu.VMEM((chans, 1, 128), F32),
            pltpu.VMEM((1, 128), F32),
            pltpu.VMEM((n_rows, 1, 128), F32),
            pltpu.VMEM((n_rows, chans, 1, 128), F32),
            pltpu.SemaphoreType.DMA((7,)),
            pltpu.SemaphoreType.REGULAR,
            pltpu.SemaphoreType.REGULAR,
            pltpu.SemaphoreType.DMA,
            pltpu.SemaphoreType.DMA((chans,)),
            pltpu.SemaphoreType.DMA((n_rows,)),
            pltpu.SemaphoreType.DMA((n_rows,)),
            pltpu.SemaphoreType.DMA,
            pltpu.SemaphoreType.DMA,
            pltpu.SemaphoreType.DMA,
            pltpu.SemaphoreType.DMA,
        ],
        compiler_params=pltpu.CompilerParams(
            collective_id=0, has_side_effects=True, vmem_limit_bytes=40 * 1024 * 1024
        ),
    )(*[pltpu.with_memory_space_constraint(a, HBM) for a in (which, *arrays)])


def body(row_cells, col_cells, visibilities, imaging_weights, taylor_weights, kernel_taps):
    arrays = (row_cells, col_cells, visibilities, imaging_weights, taylor_weights.T, kernel_taps)
    chans, n_rows = lax.axis_size("chan"), lax.axis_size("rows")
    width = NCOL // chans

    def more(state):
        return state[0] < state[1]

    def step(state):
        done, _, total = state
        part, rounds = grid_round(chans, n_rows, width, done[None], arrays)
        return done + 1, rounds[0], total + part

    part, rounds = grid_round(chans, n_rows, width, jnp.zeros((1,), jnp.int32), arrays)
    _, _, total = lax.while_loop(more, step, (jnp.int32(1), rounds[0], part))
    return total.reshape(width, TERMS, 2, ROWS_DEV)


def solution(mesh):
    in_specs = (
        P("chan", "rows"),
        P("chan", "rows"),
        P("chan", None, "rows"),
        P("chan", "rows"),
        P("chan", None),
        P(),
    )
    out_specs = P("chan", None, None, "rows")
    return jax.shard_map(body, mesh=mesh, in_specs=in_specs, out_specs=out_specs, check_vma=False)
```
